128 devices in a mesh: space: 64 (over z, y, x), mode: 2 (over core).
Axes of the slice: x: 4, y: 4, z: 4, core: 2. Of those that a mesh axis runs over, the one named last changes fastest.
Arguments:
- basis: float32 [256, 524288], P('mode', 'space'), as said below
- adjoint: float32 [256, 524288], P('mode', 'space'), as said below
- snapshots: float32 [32, 524288], P('mode', 'space'), as said below
- volumes: float32 [524288], P('space'), may hold values from 0.5 to 2, as said below
- singular: float32 [256], replicated, may hold values from 1 to 4
Outputs:
- new_basis: float32 [256, 524288], P('mode', 'space')
- new_singular: float32 [256], P('mode')
- hankel: float32 [256, 256], P('mode')
The draws below stay inside these ranges and needn't reach their ends.
Inputs may be any that keep to these rules, and one draw needn't show every extreme that they name: `basis`: real values. `adjoint`: real values. `snapshots`: real values. Positive cell volumes.
All inputs are finite; a program needn't handle non-finite values.
Results may differ from the reference program's by a relative error of at most 0.00007.
Values sent between devices are 32-bit elements; how exact they have to be, the bound alone decides.
A program may use at most 128 MiB of HBM per device.

```python
import math
import jax
import jax.numpy as jnp
from jax import lax

MODES = 256
SNAPS = 32
ROWS = 524288


mixing_terms = 8


drift_terms = 4


def volume_field(key):
    volume_key = jax.random.fold_in(key, 41)
    return jnp.exp(jax.random.uniform(volume_key, (ROWS,), jnp.float32, math.log(0.5), math.log(2.0)))


def cosine_field(key):
    row_total = ROWS
    frequencies = jax.random.permutation(jax.random.fold_in(key, 12), row_total - 1)[:MODES] + 1
    places = jax.random.permutation(jax.random.fold_in(key, 13), row_total)
    sign_flip = 2 * jax.random.randint(jax.random.fold_in(key, 14), (row_total,), 0, 2) - 1
    period = 4 * row_total
    odd_place = 2 * places + 1
    low_bits = frequencies % 1024
    high_bits = frequencies // 1024
    low_phase = odd_place[None, :] * low_bits[:, None] % period
    high_phase = odd_place[None, :] * high_bits[:, None] % period
    high_phase = high_phase * 32 % period
    high_phase = high_phase * 32 % period
    phases = (low_phase + high_phase) % period
    angles = phases.astype(jnp.float32) * (math.pi / (2.0 * row_total))
    values = math.sqrt(2.0) * jnp.cos(angles)
    column_scale = sign_flip.astype(jnp.float32) / jnp.sqrt(volume_field(key))
    return values * column_scale[None, :]


def basis_field(key):
    pure_field = cosine_field(key)
    partners = jax.random.randint(jax.random.fold_in(key, 15), (MODES, drift_terms), 0, MODES)
    drift = jnp.clip(jax.random.normal(jax.random.fold_in(key, 16), (MODES, drift_terms), jnp.float32), -3.0, 3.0) * 0.03
    result = pure_field
    for position in range(drift_terms):
        result = result + drift[:, position:position + 1] * pure_field[partners[:, position]]
    return result


def mixture(key, offset_salt, count_rows, term_count):
    modes_field = basis_field(key)
    chosen = jax.random.randint(jax.random.fold_in(key, offset_salt), (count_rows, term_count), 0, MODES)
    weights = jnp.clip(jax.random.normal(jax.random.fold_in(key, offset_salt + 1), (count_rows, term_count), jnp.float32), -3.0, 3.0) * 0.5
    result = jnp.clip(jax.random.normal(jax.random.fold_in(key, offset_salt + 2), (count_rows, ROWS), jnp.float32), -4.5, 4.5)
    for position in range(term_count):
        result = result + weights[:, position:position + 1] * modes_field[chosen[:, position]]
    return result


def draw_basis(key, part):
    return basis_field(key)


def draw_snapshots(key, part):
    return mixture(key, 20, SNAPS, mixing_terms)


def draw_adjoint(key, part):
    return mixture(key, 30, MODES, 2)


def draw_volumes(key, part):
    return volume_field(key)


def setup_inputs(seed: int = 0) -> dict:
    seeds = jax.random.split(jax.random.key(seed), 6)
    return {
        "basis": draw_basis(jax.random.fold_in(seeds[5], 71), 0),
        "adjoint": draw_adjoint(jax.random.fold_in(seeds[5], 71), 0),
        "snapshots": draw_snapshots(jax.random.fold_in(seeds[5], 71), 0),
        "volumes": draw_volumes(jax.random.fold_in(seeds[5], 71), 0),
        "singular": jnp.clip(jnp.exp(jax.random.uniform(seeds[4], (MODES,), jnp.float32, math.log(1.0), math.log(4.0))), 1.0, 4.0),
    }


highest = lax.Precision.HIGHEST

def invert_lower(lower_factor):
    identity = jnp.eye(lower_factor.shape[0], dtype=lower_factor.dtype)
    return lax.linalg.triangular_solve(lower_factor, identity, left_side=True, lower=True)

def orthonormal(gram, row_block):
    lower_factor = jnp.linalg.cholesky(gram)
    return (lower_factor, jnp.dot(invert_lower(lower_factor), row_block, precision=highest))

def truncate(singular, project, triangle):
    full_width = singular.shape[0]
    snap_count = triangle.shape[0]
    upper_rows = jnp.concatenate([jnp.diag(singular), project], axis=1)
    lower_rows = jnp.concatenate([jnp.zeros((snap_count, full_width), singular.dtype), triangle.T], axis=1)
    core_matrix = jnp.concatenate([upper_rows, lower_rows], axis=0)
    square = jnp.dot(core_matrix, core_matrix.T, precision=highest)
    leading = square[:, :full_width]
    lead_lower = jnp.linalg.cholesky(jnp.dot(leading.T, leading, precision=highest))
    rotate = jnp.dot(leading, invert_lower(lead_lower).T, precision=highest)
    energy = lax.optimization_barrier(jnp.sum(rotate * jnp.dot(square, rotate, precision=highest), axis=0))
    return (rotate, jnp.sqrt(energy))

def reference(basis, adjoint, snapshots, volumes, singular):
    scaled = volumes / ROWS
    project = jnp.dot(basis, (snapshots * scaled).T, precision=highest)
    residual = snapshots - jnp.dot(project.T, basis, precision=highest)
    gram_one = jnp.dot(residual * scaled, residual.T, precision=highest)
    triangle, ortho = orthonormal(gram_one, residual)
    rotate, new_singular = truncate(singular, project, triangle)
    new_basis = jnp.dot(rotate[:MODES].T, basis, precision=highest) + jnp.dot(rotate[MODES:].T, ortho, precision=highest)
    hankel = jnp.dot(new_basis * scaled, adjoint.T, precision=highest)
    return (new_basis, new_singular, hankel)
```

```python
import functools

import jax
import jax.numpy as jnp
from jax import lax
from jax.experimental import pallas as pl
from jax.experimental.pallas import tpu as pltpu
from jax.sharding import PartitionSpec as P

MESH = pl.DeviceIdType.MESH
highest = lax.Precision.HIGHEST
f32 = jnp.float32
bf16 = jnp.bfloat16
SIDE = 4
CHUNK = 1024


def split(value):
    high = value.astype(bf16)
    return high, (value - high.astype(f32)).astype(bf16)


def dot_nt(left, right):
    return lax.dot_general(left, right, (((1,), (1,)), ((), ())), preferred_element_type=f32)


def dot3(left, right):
    return dot_nt(left[0], right[0]) + (dot_nt(left[0], right[1]) + dot_nt(left[1], right[0]))


def exact_nt(left, right):
    return lax.dot_general(
        left, right, (((1,), (1,)), ((), ())), precision=highest, preferred_element_type=f32
    )


def exact_nn(left, right):
    return lax.dot_general(
        left, right, (((1,), (0,)), ((), ())), precision=highest, preferred_element_type=f32
    )


def gather_kernel(
    cells,
    basis, adjoint, snaps, volumes,
    other_out, snaps_out, project_out, gram_out, cross_out,
    own, other, adj, snap, root,
    own_hi, own_lo, adj_hi, adj_lo,
    acc_own, acc_other, cross,
    p_val, p_x, p_y, p_z, w_val, w_x, w_y, w_z, h_val, h_x, h_y, h_z, h_all,
    load_sem, adj_sem, small_sem, bs_sem, br_sem, ss_sem, out_sem,
    ps_sem, pr_sem, ws_sem, wr_sem, hs_sem, hr_sem,
):
    tile, width = own.shape
    snap_count = snap.shape[0]
    half = snap_count // 2
    chunks = width // CHUNK
    place = lax.axis_index("space")
    core = lax.axis_index("mode")
    peer_core = 1 - core
    x = lax.rem(place, SIDE)
    y = lax.rem(place // SIDE, SIDE)
    z = place // (SIDE * SIDE)

    def along(axis, step):
        if axis == "x":
            return place - x + lax.rem(x + step, SIDE)
        if axis == "y":
            return place + (lax.rem(y + step, SIDE) - y) * SIDE
        return place + (lax.rem(z + step, SIDE) - z) * (SIDE * SIDE)

    snap_rows = pl.ds(pl.multiple_of(core * half, half), half)
    load_snap = pltpu.make_async_copy(snaps, snap.at[snap_rows], small_sem.at[0])
    load_snap.start()

    def piece(k):
        return pl.ds(pl.multiple_of(k * CHUNK, CHUNK), CHUNK)

    def load_own(k):
        return pltpu.make_async_copy(basis.at[:, piece(k)], own.at[:, piece(k)], load_sem.at[k])

    def load_adj(k):
        return pltpu.make_async_copy(adjoint.at[:, piece(k)], adj.at[:, piece(k)], adj_sem.at[k])

    for k in range(chunks):
        load_own(k).start()
    for k in range(chunks):
        load_adj(k).start()

    barrier = pltpu.get_barrier_semaphore()
    friends = [(place, peer_core)]
    for step in range(1, SIDE):
        friends += [(along(axis, step), core) for axis in "xyz"]
        friends += [(along(axis, step), peer_core) for axis in "xz"]
    for friend in friends:
        pl.semaphore_signal(barrier, inc=1, device_id=friend, device_id_type=MESH)
    pl.semaphore_wait(barrier, len(friends))

    pair = (place, peer_core)

    def remote(src, dst, send_sem, recv_sem, device):
        return pltpu.make_async_remote_copy(
            src_ref=src, dst_ref=dst, send_sem=send_sem, recv_sem=recv_sem,
            device_id=device, device_id_type=MESH,
        )

    send_snap = remote(snaps, snap.at[snap_rows], ss_sem.at[0], ss_sem.at[1], pair)
    send_snap.start()

    def send_own(k):
        return remote(basis.at[:, piece(k)], other.at[:, piece(k)], bs_sem.at[k], br_sem.at[k], pair)

    for k in range(chunks):
        send_own(k).start()

    root[...] = jnp.sqrt(volumes[...] * (1.0 / cells))
    load_snap.wait()
    send_snap.wait()
    save_snap = pltpu.make_async_copy(snap, snaps_out, out_sem.at[0])
    save_snap.start()

    acc_own[...] = jnp.zeros_like(acc_own)
    acc_other[...] = jnp.zeros_like(acc_other)

    def first(k, carry):
        load_own(k).wait()
        cols = piece(k)
        rows = jnp.concatenate([own[:, cols], snap[:, cols]], axis=0) * root[:, cols]
        parts = split(rows)
        own_hi[:, cols], own_lo[:, cols] = parts
        acc_own[:, : tile + snap_count] += dot3(parts, parts)
        return carry

    lax.fori_loop(0, chunks, first, 0)

    def sends(src, buf, axis, send_sem, recv_sem, base, across):
        copies = []
        for step in range(1, SIDE):
            slot = base + step
            dst = buf.at[0, step] if across else buf.at[step]
            copies.append(
                remote(src, dst, send_sem.at[slot], recv_sem.at[slot], (along(axis, step), core))
            )
        if across:
            for step in range(SIDE):
                slot = base + SIDE + step
                copies.append(
                    remote(src, buf.at[1, step], send_sem.at[slot], recv_sem.at[slot],
                           (along(axis, step), peer_core))
                )
        for copy in copies:
            copy.start()
        return copies

    def waits(copies):
        for copy in copies:
            copy.wait()

    def four(value, buf):
        return (value + buf[2]) + (buf[1] + buf[3])

    p_val[0] = acc_own[tile : tile + snap_count, :tile]
    copies = sends(p_val.at[0], p_x, "x", ps_sem, pr_sem, 0, False)

    def second(k, carry):
        load_adj(k).wait()
        cols = piece(k)
        parts = split(adj[:, cols] * root[:, cols])
        adj_hi[:, cols], adj_lo[:, cols] = parts
        value = dot3((own_hi[:, cols], own_lo[:, cols]), parts)
        cross[:tile] += value[:tile]
        cross[2 * tile :] += value[tile:]
        return carry

    cross[...] = jnp.zeros_like(cross)
    lax.fori_loop(0, chunks, second, 0)

    waits(copies)
    p_val[1] = four(p_val[0], p_x)
    copies = sends(p_val.at[1], p_y, "y", ps_sem, pr_sem, SIDE, False)

    def third(k, carry):
        send_own(k).wait_recv()
        cols = piece(k)
        pltpu.make_async_copy(other.at[:, cols], other_out.at[:, cols], out_sem.at[k + 1]).start()
        left = split(other[:, cols] * root[:, cols])
        right = tuple(
            jnp.concatenate([a[:, cols], b[:tile, cols]], axis=0)
            for a, b in ((adj_hi, own_hi), (adj_lo, own_lo))
        )
        acc_other[...] += dot3(left, right)
        return carry

    lax.fori_loop(0, chunks // 2, third, 0)
    waits(copies)
    p_val[2] = four(p_val[1], p_y)
    copies = sends(p_val.at[2], p_z, "z", ps_sem, pr_sem, 2 * SIDE, True)
    lax.fori_loop(chunks // 2, chunks, third, 0)

    cross[tile : 2 * tile] = acc_other[:, :tile]
    quarter = cross.shape[0] // SIDE

    def quarter_rows(which):
        return pl.ds(pl.multiple_of(which * quarter, 8), quarter)

    h_copies = []
    for step in range(1, SIDE):
        h_copies.append(
            remote(cross.at[quarter_rows(lax.rem(x + step, SIDE))], h_x.at[step],
                   hs_sem.at[step], hr_sem.at[step], (along("x", step), core))
        )
        h_copies[-1].start()

    waits(copies)
    p_own = four(p_val[2], p_z.at[0])
    p_other = (p_z[1, 0] + p_z[1, 2]) + (p_z[1, 1] + p_z[1, 3])
    first_core = core == 0
    project_out[0] = jnp.where(first_core, p_own, p_other)
    project_out[1] = jnp.where(first_core, p_other, p_own)

    mixed = exact_nn(p_own, acc_own[:tile, :tile]) + exact_nn(p_other, acc_other[:, tile:])
    share = exact_nt(mixed, p_own) + 0.5 * acc_own[tile : tile + snap_count, tile : tile + snap_count]
    w_val[0] = jnp.concatenate([share, jnp.zeros((snap_count, tile - snap_count), f32)], axis=1)
    copies = sends(w_val.at[0], w_x, "x", ws_sem, wr_sem, 0, False)
    twice = 2.0 * (exact_nt(project_out[0], project_out[0]) + exact_nt(project_out[1], project_out[1]))

    waits(copies)
    w_val[1] = four(w_val[0], w_x)
    copies = sends(w_val.at[1], w_y, "y", ws_sem, wr_sem, SIDE, False)

    waits(h_copies)
    h_val[0] = four(cross[quarter_rows(x)], h_x)
    h_copies = sends(h_val.at[0], h_y, "y", hs_sem, hr_sem, SIDE, False)

    waits(copies)
    w_val[2] = four(w_val[1], w_y)
    copies = sends(w_val.at[2], w_z, "z", ws_sem, wr_sem, 2 * SIDE, True)

    waits(h_copies)
    h_val[1] = four(h_val[0], h_y)
    h_copies = sends(h_val.at[1], h_z, "z", hs_sem, hr_sem, 2 * SIDE, False)

    waits(copies)
    w_own = four(w_val[2], w_z.at[0])
    w_other = (w_z[1, 0] + w_z[1, 2]) + (w_z[1, 1] + w_z[1, 3])
    gram_out[...] = (w_own + w_other)[:, :snap_count] - twice

    waits(h_copies)
    h_val[2] = four(h_val[1], h_z)
    h_copies = []
    for side in range(2):
        for step in range(1 - side, SIDE):
            slot = 3 * SIDE + side * SIDE + step
            h_copies.append(
                remote(h_val.at[2], h_all.at[side, quarter_rows(x)],
                       hs_sem.at[slot], hr_sem.at[slot],
                       (along("x", step), core if side == 0 else peer_core))
            )
            h_copies[-1].start()
    h_index = 0
    for side in range(2):
        for step in range(1 - side, SIDE):
            slot = 3 * SIDE + side * SIDE + step
            h_copies[h_index].wait_send()
            h_index += 1
            sender = lax.rem(x + SIDE - step, SIDE)
            remote(h_val.at[2], h_all.at[side, quarter_rows(sender)],
                   hs_sem.at[slot], hr_sem.at[slot], pair).wait_recv()
    h_all[0, quarter_rows(x)] = h_val[2]
    cross_out[...] = h_all[...]

    def finish(k, carry):
        send_own(k).wait_send()
        pltpu.make_async_copy(other.at[:, piece(k)], other_out.at[:, piece(k)], out_sem.at[k + 1]).wait()
        return carry

    lax.fori_loop(0, chunks, finish, 0)
    save_snap.wait()


def gather(cells, basis, adjoint, snapshots, volumes):
    tile, width = basis.shape
    snap_count = 2 * snapshots.shape[0]
    rows = 2 * tile + snap_count
    quarter = rows // SIDE
    chunks = width // CHUNK
    dma = pltpu.SemaphoreType.DMA
    vmem = pltpu.VMEM
    any_spec = pl.BlockSpec(memory_space=pl.ANY)
    vmem_spec = pl.BlockSpec(memory_space=vmem)
    return pl.pallas_call(
        functools.partial(gather_kernel, cells),
        out_shape=(
            jax.ShapeDtypeStruct((tile, width), f32),
            jax.ShapeDtypeStruct((snap_count, width), f32),
            jax.ShapeDtypeStruct((2, snap_count, tile), f32),
            jax.ShapeDtypeStruct((snap_count, snap_count), f32),
            jax.ShapeDtypeStruct((2, rows, tile), f32),
        ),
        in_specs=[any_spec, any_spec, any_spec, vmem_spec],
        out_specs=(any_spec, any_spec, vmem_spec, vmem_spec, vmem_spec),
        scratch_shapes=[
            vmem((tile, width), f32),
            vmem((tile, width), f32),
            vmem((tile, width), f32),
            vmem((snap_count, width), f32),
            vmem((1, width), f32),
            vmem((tile + snap_count, width), bf16),
            vmem((tile + snap_count, width), bf16),
            vmem((tile, width), bf16),
            vmem((tile, width), bf16),
            vmem((tile + snap_count, 2 * tile), f32),
            vmem((tile, 2 * tile), f32),
            vmem((rows, tile), f32),
            vmem((3, snap_count, tile), f32),
            vmem((SIDE, snap_count, tile), f32),
            vmem((SIDE, snap_count, tile), f32),
            vmem((2, SIDE, snap_count, tile), f32),
            vmem((3, snap_count, tile), f32),
            vmem((SIDE, snap_count, tile), f32),
            vmem((SIDE, snap_count, tile), f32),
            vmem((2, SIDE, snap_count, tile), f32),
            vmem((3, quarter, tile), f32),
            vmem((SIDE, quarter, tile), f32),
            vmem((SIDE, quarter, tile), f32),
            vmem((SIDE, quarter, tile), f32),
            vmem((2, rows, tile), f32),
            dma((chunks,)),
            dma((chunks,)),
            dma((1,)),
            dma((chunks,)),
            dma((chunks,)),
            dma((2,)),
            dma((chunks + 1,)),
            dma((4 * SIDE,)),
            dma((4 * SIDE,)),
            dma((4 * SIDE,)),
            dma((4 * SIDE,)),
            dma((5 * SIDE,)),
            dma((5 * SIDE,)),
        ],
        compiler_params=pltpu.CompilerParams(
            collective_id=0, has_side_effects=True, vmem_limit_bytes=56 * 1024 * 1024
        ),
    )(basis, adjoint, snapshots, volumes)


def invert_lower(lower_factor):
    identity = jnp.eye(lower_factor.shape[0], dtype=lower_factor.dtype)
    return lax.linalg.triangular_solve(lower_factor, identity, left_side=True, lower=True)


def shards(basis, adjoint, snapshots, volumes, singular):
    tile, width = basis.shape
    core = lax.axis_index("mode")
    cells = float(width * lax.axis_size("space"))
    other, snaps, project_t, gram, cross = gather(
        cells, basis, adjoint, snapshots, volumes.reshape(1, width)
    )
    project = jnp.concatenate([project_t[0], project_t[1]], axis=1).T
    first_core = core == 0

    def ordered(mine, others):
        return jnp.where(first_core, mine, others), jnp.where(first_core, others, mine)

    swapped = jnp.concatenate([cross[1, tile : 2 * tile], cross[1, :tile], cross[1, 2 * tile :]], axis=0)
    left, right = ordered(cross[0], swapped)
    cross = jnp.concatenate([left, right], axis=1)
    top, bottom = ordered(cross[:tile], cross[tile : 2 * tile])
    squares = singular * singular
    core_top = jnp.diag(squares) + jnp.dot(project, project.T, precision=highest)
    core_side = jnp.dot(core_top, project, precision=highest) + jnp.dot(project, gram, precision=highest)
    gram_lead = core_top * squares + jnp.dot(core_side, project.T, precision=highest)
    gram_lead = 0.5 * (gram_lead + gram_lead.T)
    inverse = invert_lower(jnp.linalg.cholesky(gram_lead))
    inverse = lax.dynamic_slice_in_dim(inverse, core * tile, tile, 0)
    energy = jnp.sum(jnp.square(jnp.dot(inverse, core_top * singular, precision=highest)), axis=1)
    energy = energy + jnp.sum(jnp.square(jnp.dot(inverse, core_side, precision=highest)), axis=1)
    on_modes = inverse * squares
    on_snaps = jnp.dot(inverse, project, precision=highest)
    hankel = (
        jnp.dot(on_modes[:, :tile], top, precision=highest)
        + jnp.dot(on_modes[:, tile:], bottom, precision=highest)
        + jnp.dot(on_snaps, cross[2 * tile :], precision=highest)
    )
    on_first, on_second = on_modes[:, :tile], on_modes[:, tile:]
    on_own, on_other = ordered(on_first, on_second)
    new_tile = (
        jnp.dot(on_own, basis, precision=highest)
        + jnp.dot(on_other, other, precision=highest)
        + jnp.dot(on_snaps, snaps, precision=highest)
    )
    return new_tile, jnp.sqrt(energy), hankel


def solution(mesh):
    return jax.shard_map(
        shards,
        mesh=mesh,
        in_specs=(P("mode", "space"), P("mode", "space"), P("mode", "space"), P("space"), P()),
        out_specs=(P("mode", "space"), P("mode"), P("mode", None)),
        check_vma=False,
    )
```

```python
import functools

import jax
import jax.numpy as jnp
from jax import lax
from jax.experimental import pallas as pl
from jax.experimental.pallas import tpu as pltpu
from jax.sharding import PartitionSpec as P

MESH = pl.DeviceIdType.MESH
highest = lax.Precision.HIGHEST
f32 = jnp.float32
bf16 = jnp.bfloat16
SIDE = 4
CHUNK = 1024


def split(value):
    high = value.astype(bf16)
    return high, (value - high.astype(f32)).astype(bf16)


def dot_nt(left, right):
    return lax.dot_general(left, right, (((1,), (1,)), ((), ())), preferred_element_type=f32)


def dot3(left, right):
    return dot_nt(left[0], right[0]) + (dot_nt(left[0], right[1]) + dot_nt(left[1], right[0]))


def exact_nt(left, right):
    return lax.dot_general(
        left, right, (((1,), (1,)), ((), ())), precision=highest, preferred_element_type=f32
    )


def exact_nn(left, right):
    return lax.dot_general(
        left, right, (((1,), (0,)), ((), ())), precision=highest, preferred_element_type=f32
    )


def gather_kernel(
    cells,
    basis, adjoint, snaps, volumes,
    other_out, snaps_out, project_out, gram_out, cross_out,
    own, other, adj, snap, root,
    own_hi, own_lo, adj_hi, adj_lo,
    acc_own, acc_other, cross,
    p_val, p_x, p_y, p_z, w_val, w_x, w_y, w_z, h_val, h_x, h_y, h_z, h_all,
    load_sem, adj_sem, small_sem, bs_sem, br_sem, ss_sem, out_sem,
    ps_sem, pr_sem, ws_sem, wr_sem, hs_sem, hr_sem,
):
    tile, width = own.shape
    snap_count = snap.shape[0]
    half = snap_count // 2
    chunks = width // CHUNK
    place = lax.axis_index("space")
    core = lax.axis_index("mode")
    peer_core = 1 - core
    x = lax.rem(place, SIDE)
    y = lax.rem(place // SIDE, SIDE)
    z = place // (SIDE * SIDE)

    def along(axis, step):
        if axis == "x":
            return place - x + lax.rem(x + step, SIDE)
        if axis == "y":
            return place + (lax.rem(y + step, SIDE) - y) * SIDE
        return place + (lax.rem(z + step, SIDE) - z) * (SIDE * SIDE)

    snap_rows = pl.ds(pl.multiple_of(core * half, half), half)
    load_snap = pltpu.make_async_copy(snaps, snap.at[snap_rows], small_sem.at[0])
    load_snap.start()

    def piece(k):
        return pl.ds(pl.multiple_of(k * CHUNK, CHUNK), CHUNK)

    def load_own(k):
        return pltpu.make_async_copy(basis.at[:, piece(k)], own.at[:, piece(k)], load_sem.at[k])

    def load_adj(k):
        return pltpu.make_async_copy(adjoint.at[:, piece(k)], adj.at[:, piece(k)], adj_sem.at[k])

    for k in range(chunks):
        load_own(k).start()
    for k in range(chunks):
        load_adj(k).start()

    barrier = pltpu.get_barrier_semaphore()
    friends = [(place, peer_core)]
    for step in range(1, SIDE):
        friends += [(along(axis, step), core) for axis in "xyz"]
        friends += [(along(axis, step), peer_core) for axis in "xz"]
    for friend in friends:
        pl.semaphore_signal(barrier, inc=1, device_id=friend, device_id_type=MESH)
    pl.semaphore_wait(barrier, len(friends))

    pair = (place, peer_core)

    def remote(src, dst, send_sem, recv_sem, device):
        return pltpu.make_async_remote_copy(
            src_ref=src, dst_ref=dst, send_sem=send_sem, recv_sem=recv_sem,
            device_id=device, device_id_type=MESH,
        )

    send_snap = remote(snaps, snap.at[snap_rows], ss_sem.at[0], ss_sem.at[1], pair)
    send_snap.start()

    def send_own(k):
        return remote(basis.at[:, piece(k)], other.at[:, piece(k)], bs_sem.at[k], br_sem.at[k], pair)

    for k in range(chunks):
        send_own(k).start()

    root[...] = jnp.sqrt(volumes[...] * (1.0 / cells))
    load_snap.wait()
    send_snap.wait()
    save_snap = pltpu.make_async_copy(snap, snaps_out, out_sem.at[0])
    save_snap.start()

    acc_own[...] = jnp.zeros_like(acc_own)
    acc_other[...] = jnp.zeros_like(acc_other)

    def first(k, carry):
        load_own(k).wait()
        cols = piece(k)
        rows = jnp.concatenate([own[:, cols], snap[:, cols]], axis=0) * root[:, cols]
        parts = split(rows)
        own_hi[:, cols], own_lo[:, cols] = parts
        acc_own[:, : tile + snap_count] += dot3(parts, parts)
        return carry

    lax.fori_loop(0, chunks, first, 0)

    def sends(src, buf, axis, send_sem, recv_sem, base, across):
        copies = []
        for step in range(1, SIDE):
            slot = base + step
            dst = buf.at[0, step] if across else buf.at[step]
            copies.append(
                remote(src, dst, send_sem.at[slot], recv_sem.at[slot], (along(axis, step), core))
            )
        if across:
            for step in range(SIDE):
                slot = base + SIDE + step
                copies.append(
                    remote(src, buf.at[1, step], send_sem.at[slot], recv_sem.at[slot],
                           (along(axis, step), peer_core))
                )
        for copy in copies:
            copy.start()
        return copies

    def waits(copies):
        for copy in copies:
            copy.wait()

    def four(value, buf):
        return (value + buf[2]) + (buf[1] + buf[3])

    p_val[0] = acc_own[tile : tile + snap_count, :tile]
    copies = sends(p_val.at[0], p_x, "x", ps_sem, pr_sem, 0, False)

    def second(k, carry):
        load_adj(k).wait()
        cols = piece(k)
        parts = split(adj[:, cols] * root[:, cols])
        adj_hi[:, cols], adj_lo[:, cols] = parts
        value = dot3((own_hi[:, cols], own_lo[:, cols]), parts)
        cross[:tile] += value[:tile]
        cross[2 * tile :] += value[tile:]
        return carry

    cross[...] = jnp.zeros_like(cross)
    lax.fori_loop(0, chunks, second, 0)

    waits(copies)
    p_val[1] = four(p_val[0], p_x)
    copies = sends(p_val.at[1], p_y, "y", ps_sem, pr_sem, SIDE, False)

    def third(k, carry):
        send_own(k).wait_recv()
        cols = piece(k)
        pltpu.make_async_copy(other.at[:, cols], other_out.at[:, cols], out_sem.at[k + 1]).start()
        left = split(other[:, cols] * root[:, cols])
        right = tuple(
            jnp.concatenate([a[:, cols], b[:tile, cols]], axis=0)
            for a, b in ((adj_hi, own_hi), (adj_lo, own_lo))
        )
        acc_other[...] += dot3(left, right)
        return carry

    lax.fori_loop(0, chunks // 2, third, 0)
    waits(copies)
    p_val[2] = four(p_val[1], p_y)
    copies = sends(p_val.at[2], p_z, "z", ps_sem, pr_sem, 2 * SIDE, True)
    lax.fori_loop(chunks // 2, chunks, third, 0)

    cross[tile : 2 * tile] = acc_other[:, :tile]
    quarter = cross.shape[0] // SIDE

    def quarter_rows(which):
        return pl.ds(pl.multiple_of(which * quarter, 8), quarter)

    h_copies = []
    for step in range(1, SIDE):
        h_copies.append(
            remote(cross.at[quarter_rows(lax.rem(x + step, SIDE))], h_x.at[step],
                   hs_sem.at[step], hr_sem.at[step], (along("x", step), core))
        )
        h_copies[-1].start()

    waits(copies)
    p_own = four(p_val[2], p_z.at[0])
    p_other = (p_z[1, 0] + p_z[1, 2]) + (p_z[1, 1] + p_z[1, 3])
    first_core = core == 0
    project_out[0] = jnp.where(first_core, p_own, p_other)
    project_out[1] = jnp.where(first_core, p_other, p_own)

    mixed = exact_nn(p_own, acc_own[:tile, :tile]) + exact_nn(p_other, acc_other[:, tile:])
    share = exact_nt(mixed, p_own) + 0.5 * acc_own[tile : tile + snap_count, tile : tile + snap_count]
    w_val[0] = jnp.concatenate([share, jnp.zeros((snap_count, tile - snap_count), f32)], axis=1)
    copies = sends(w_val.at[0], w_x, "x", ws_sem, wr_sem, 0, False)
    twice = 2.0 * (exact_nt(project_out[0], project_out[0]) + exact_nt(project_out[1], project_out[1]))

    waits(copies)
    w_val[1] = four(w_val[0], w_x)
    copies = sends(w_val.at[1], w_y, "y", ws_sem, wr_sem, SIDE, False)

    waits(h_copies)
    h_val[0] = four(cross[quarter_rows(x)], h_x)
    h_copies = sends(h_val.at[0], h_y, "y", hs_sem, hr_sem, SIDE, False)

    waits(copies)
    w_val[2] = four(w_val[1], w_y)
    copies = sends(w_val.at[2], w_z, "z", ws_sem, wr_sem, 2 * SIDE, True)

    waits(h_copies)
    h_val[1] = four(h_val[0], h_y)
    h_copies = sends(h_val.at[1], h_z, "z", hs_sem, hr_sem, 2 * SIDE, False)

    waits(copies)
    w_own = four(w_val[2], w_z.at[0])
    w_other = (w_z[1, 0] + w_z[1, 2]) + (w_z[1, 1] + w_z[1, 3])
    gram_out[...] = (w_own + w_other)[:, :snap_count] - twice

    waits(h_copies)
    h_val[2] = four(h_val[1], h_z)
    h_copies = []
    for side in range(2):
        for step in range(1 - side, SIDE):
            slot = 3 * SIDE + side * SIDE + step
            h_copies.append(
                remote(h_val.at[2], h_all.at[side, quarter_rows(x)],
                       hs_sem.at[slot], hr_sem.at[slot],
                       (along("x", step), core if side == 0 else peer_core))
            )
            h_copies[-1].start()
    h_index = 0
    for side in range(2):
        for step in range(1 - side, SIDE):
            slot = 3 * SIDE + side * SIDE + step
            h_copies[h_index].wait_send()
            h_index += 1
            sender = lax.rem(x + SIDE - step, SIDE)
            remote(h_val.at[2], h_all.at[side, quarter_rows(sender)],
                   hs_sem.at[slot], hr_sem.at[slot], pair).wait_recv()
    h_all[0, quarter_rows(x)] = h_val[2]
    cross_out[...] = h_all[...]

    def finish(k, carry):
        send_own(k).wait_send()
        pltpu.make_async_copy(other.at[:, piece(k)], other_out.at[:, piece(k)], out_sem.at[k + 1]).wait()
        return carry

    lax.fori_loop(0, chunks, finish, 0)
    save_snap.wait()


def gather(cells, basis, adjoint, snapshots, volumes):
    tile, width = basis.shape
    snap_count = 2 * snapshots.shape[0]
    rows = 2 * tile + snap_count
    quarter = rows // SIDE
    chunks = width // CHUNK
    dma = pltpu.SemaphoreType.DMA
    vmem = pltpu.VMEM
    any_spec = pl.BlockSpec(memory_space=pl.ANY)
    vmem_spec = pl.BlockSpec(memory_space=vmem)
    return pl.pallas_call(
        functools.partial(gather_kernel, cells),
        out_shape=(
            jax.ShapeDtypeStruct((tile, width), f32),
            jax.ShapeDtypeStruct((snap_count, width), f32),
            jax.ShapeDtypeStruct((2, snap_count, tile), f32),
            jax.ShapeDtypeStruct((snap_count, snap_count), f32),
            jax.ShapeDtypeStruct((2, rows, tile), f32),
        ),
        in_specs=[any_spec, any_spec, any_spec, vmem_spec],
        out_specs=(any_spec, any_spec, vmem_spec, vmem_spec, vmem_spec),
        scratch_shapes=[
            vmem((tile, width), f32),
            vmem((tile, width), f32),
            vmem((tile, width), f32),
            vmem((snap_count, width), f32),
            vmem((1, width), f32),
            vmem((tile + snap_count, width), bf16),
            vmem((tile + snap_count, width), bf16),
            vmem((tile, width), bf16),
            vmem((tile, width), bf16),
            vmem((tile + snap_count, 2 * tile), f32),
            vmem((tile, 2 * tile), f32),
            vmem((rows, tile), f32),
            vmem((3, snap_count, tile), f32),
            vmem((SIDE, snap_count, tile), f32),
            vmem((SIDE, snap_count, tile), f32),
            vmem((2, SIDE, snap_count, tile), f32),
            vmem((3, snap_count, tile), f32),
            vmem((SIDE, snap_count, tile), f32),
            vmem((SIDE, snap_count, tile), f32),
            vmem((2, SIDE, snap_count, tile), f32),
            vmem((3, quarter, tile), f32),
            vmem((SIDE, quarter, tile), f32),
            vmem((SIDE, quarter, tile), f32),
            vmem((SIDE, quarter, tile), f32),
            vmem((2, rows, tile), f32),
            dma((chunks,)),
            dma((chunks,)),
            dma((1,)),
            dma((chunks,)),
            dma((chunks,)),
            dma((2,)),
            dma((chunks + 1,)),
            dma((4 * SIDE,)),
            dma((4 * SIDE,)),
            dma((4 * SIDE,)),
            dma((4 * SIDE,)),
            dma((5 * SIDE,)),
            dma((5 * SIDE,)),
        ],
        compiler_params=pltpu.CompilerParams(
            collective_id=0, has_side_effects=True, vmem_limit_bytes=56 * 1024 * 1024
        ),
    )(basis, adjoint, snapshots, volumes)


def dot_nn(left, right):
    return lax.dot_general(left, right, (((1,), (0,)), ((), ())), preferred_element_type=f32)


def dot3_nn(left, right):
    rows = left[0].shape[0]
    both = dot_nn(jnp.concatenate([left[0], left[1]], axis=0), right[0])
    return both[:rows] + (dot_nn(left[0], right[1]) + both[rows:])


def exact_tn(left, right):
    return lax.dot_general(
        left, right, (((0,), (0,)), ((), ())), precision=highest, preferred_element_type=f32
    )


def inverse_factor(block, group):
    size = block.shape[0]
    eye = (
        lax.broadcasted_iota(jnp.int32, (size, size), 0)
        == lax.broadcasted_iota(jnp.int32, (size, size), 1)
    ).astype(f32)
    left = jnp.concatenate([block, eye], axis=1)
    done = []
    for start in range(0, size, group):
        count = size - start
        row = lax.broadcasted_iota(jnp.int32, (count, 2 * size), 0)
        cols = [
            jnp.broadcast_to(left[:, start + t : start + t + 1], (count, 2 * size))
            for t in range(group)
        ]
        for t in range(group):
            pivot = cols[t][t : t + 1, :]
            factor = jnp.where(row > t, cols[t], 0.0) * (1.0 / pivot)
            for u in range(t + 1, group):
                cols[u] = cols[u] - factor * cols[u][t : t + 1, :]
            done.append(left[t : t + 1, :] * lax.rsqrt(pivot))
            left = left - factor * left[t : t + 1, :]
        left = left[group:]
    return jnp.concatenate(done, axis=0)[:, size:]


def rotate_kernel(
    basis, other, snaps, project, gram, cross, singular,
    new_out, singular_out, hankel_out,
    rows, result, lead, inverse, coef_hi, coef_lo, in_sem, out_sem,
):
    tile, width = result.shape
    modes = 2 * tile
    snap_count = snaps.shape[0]
    chunks = width // CHUNK
    core = lax.axis_index("mode")
    first_core = core == 0

    def piece(k):
        return pl.ds(pl.multiple_of(k * CHUNK, CHUNK), CHUNK)

    def loads(k):
        cols = piece(k)
        return (
            pltpu.make_async_copy(basis.at[:, cols], rows.at[:tile, cols], in_sem.at[0, k]),
            pltpu.make_async_copy(other.at[:, cols], rows.at[tile:modes, cols], in_sem.at[1, k]),
            pltpu.make_async_copy(snaps.at[:, cols], rows.at[modes:, cols], in_sem.at[2, k]),
        )

    for k in range(chunks):
        for copy in loads(k):
            copy.start()

    s = singular[...]
    s2 = s * s
    project_t = jnp.concatenate([project[0], project[1]], axis=1)
    scaled_t = project_t * s2
    pad = jnp.zeros((tile - 2 * snap_count, modes), f32)
    turned = jnp.concatenate([project_t, scaled_t, pad], axis=0).T
    by_mode, by_mode_scaled = turned[:, :snap_count], turned[:, snap_count : 2 * snap_count]
    inner = exact_nt(project_t, project_t) + gram[...]
    side = by_mode_scaled + exact_nn(by_mode, inner)
    side_and_project = jnp.concatenate([side, by_mode], axis=1)
    eye = lax.broadcasted_iota(jnp.int32, (modes, modes), 0) == lax.broadcasted_iota(
        jnp.int32, (modes, modes), 1
    )
    lead[...] = jnp.where(eye, s2 * s2, 0.0) + exact_nt(
        side_and_project, turned[:, : 2 * snap_count]
    )
    inverse[...] = eye.astype(f32)
    size = 64
    for start in range(0, modes, size):
        stop = start + size
        small = inverse_factor(lead[start:stop, start:stop], 8)
        part = exact_nn(small, inverse[start:stop, :])
        inverse[start:stop, :] = part
        if stop < modes:
            upper = exact_nn(small, lead[start:stop, :])
            later = upper[:, stop:]
            lead[stop:, :] -= exact_tn(later, upper)
            inverse[stop:, :] -= exact_tn(later, part)

    mine = inverse[pl.ds(pl.multiple_of(core * tile, tile), tile), :]
    both = exact_nn(mine, side_and_project)
    on_snaps = both[:, snap_count:]
    on_modes = mine * s2
    image = (on_modes + exact_nn(on_snaps, project_t)) * s
    energy = exact_nt(jnp.ones((8, modes), f32), image * image) + exact_nt(
        jnp.ones((8, snap_count), f32), both[:, :snap_count] * both[:, :snap_count]
    )
    singular_out[...] = jnp.sqrt(energy[:1])

    on_first, on_second = on_modes[:, :tile], on_modes[:, tile:]
    coef = split(
        jnp.concatenate(
            [
                jnp.where(first_core, on_first, on_second),
                jnp.where(first_core, on_second, on_first),
                on_snaps,
            ],
            axis=1,
        )
    )
    coef_hi[...], coef_lo[...] = coef

    def rotate(k, carry):
        for copy in loads(k):
            copy.wait()
        cols = piece(k)
        result[:, cols] = dot3_nn((coef_hi[...], coef_lo[...]), split(rows[:, cols]))
        pltpu.make_async_copy(result.at[:, cols], new_out.at[:, cols], out_sem.at[k]).start()
        return carry

    lax.fori_loop(0, chunks, rotate, 0)

    swapped = jnp.concatenate([cross[1, tile:modes], cross[1, :tile], cross[1, modes:]], axis=0)
    columns = jnp.concatenate(
        [jnp.where(first_core, cross[0], swapped), jnp.where(first_core, swapped, cross[0])], axis=1
    )
    hankel_out[...] = dot3_nn(coef, split(columns))

    def finish(k, carry):
        pltpu.make_async_copy(result.at[:, piece(k)], new_out.at[:, piece(k)], out_sem.at[k]).wait()
        return carry

    lax.fori_loop(0, chunks, finish, 0)


def rotate(basis, other, snaps, project, gram, cross, singular):
    tile, width = basis.shape
    modes, snap_count = 2 * tile, snaps.shape[0]
    chunks = width // CHUNK
    dma = pltpu.SemaphoreType.DMA
    vmem = pltpu.VMEM
    any_spec = pl.BlockSpec(memory_space=pl.ANY)
    vmem_spec = pl.BlockSpec(memory_space=vmem)
    return pl.pallas_call(
        rotate_kernel,
        out_shape=(
            jax.ShapeDtypeStruct((tile, width), f32),
            jax.ShapeDtypeStruct((1, tile), f32),
            jax.ShapeDtypeStruct((tile, modes), f32),
        ),
        in_specs=[any_spec] * 3 + [vmem_spec] * 4,
        out_specs=(any_spec, vmem_spec, vmem_spec),
        scratch_shapes=[
            vmem((modes + snap_count, width), f32),
            vmem((tile, width), f32),
            vmem((modes, modes), f32),
            vmem((modes, modes), f32),
            vmem((tile, modes + snap_count), bf16),
            vmem((tile, modes + snap_count), bf16),
            dma((3, chunks)),
            dma((chunks,)),
        ],
        compiler_params=pltpu.CompilerParams(vmem_limit_bytes=56 * 1024 * 1024),
    )(basis, other, snaps, project, gram, cross, singular)


def shards(basis, adjoint, snapshots, volumes, singular):
    tile, width = basis.shape
    cells = float(width * lax.axis_size("space"))
    other, snaps, project, gram, cross = gather(
        cells, basis, adjoint, snapshots, volumes.reshape(1, width)
    )
    new_tile, new_singular, hankel = rotate(
        basis, other, snaps, project, gram, cross, singular.reshape(1, 2 * tile)
    )
    return new_tile, new_singular.reshape(tile), hankel


def solution(mesh):
    return jax.shard_map(
        shards,
        mesh=mesh,
        in_specs=(P("mode", "space"), P("mode", "space"), P("mode", "space"), P("space"), P()),
        out_specs=(P("mode", "space"), P("mode"), P("mode", None)),
        check_vma=False,
    )
```

```python
import functools

import jax
import jax.numpy as jnp
from jax import lax
from jax.experimental import pallas as pl
from jax.experimental.pallas import tpu as pltpu
from jax.sharding import PartitionSpec as P

MESH = pl.DeviceIdType.MESH
highest = lax.Precision.HIGHEST
f32 = jnp.float32
bf16 = jnp.bfloat16
SIDE = 4
PLANE = SIDE * SIDE
CHUNK = 1024


def split(value):
    high = value.astype(bf16)
    return high, (value - high.astype(f32)).astype(bf16)


def dot_nt(left, right):
    return lax.dot_general(left, right, (((1,), (1,)), ((), ())), preferred_element_type=f32)


def dot3(left, right):
    return dot_nt(left[0], right[0]) + (dot_nt(left[0], right[1]) + dot_nt(left[1], right[0]))


def exact_nt(left, right):
    return lax.dot_general(
        left, right, (((1,), (1,)), ((), ())), precision=highest, preferred_element_type=f32
    )


def exact_nn(left, right):
    return lax.dot_general(
        left, right, (((1,), (0,)), ((), ())), precision=highest, preferred_element_type=f32
    )


def gather_kernel(
    cells,
    basis, adjoint, snaps, volumes,
    other_out, snaps_out, total_out,
    own, other, adj, snap, root,
    left_hi, left_lo, adj_hi, adj_lo,
    acc, acc_snap, share, slots, part, z_slots, total,
    load_sem, adj_sem, small_sem, bs_sem, br_sem, ss_sem, out_sem,
    rs_sem, rr_sem, zs_sem, zr_sem, gs_sem, gr_sem, fs_sem, fr_sem,
):
    tile, width = own.shape
    snap_count = snap.shape[0]
    half = snap_count // 2
    chunks = width // CHUNK
    near = tile + snap_count
    place = lax.axis_index("space")
    core = lax.axis_index("mode")
    pair = (place, 1 - core)
    spot = lax.rem(place, PLANE)
    level = place // PLANE

    def in_plane(step):
        return lax.rem(spot + step, PLANE)

    def plane_peer(step):
        return (level * PLANE + in_plane(step), core)

    def level_peer(step):
        return (lax.rem(level + step, SIDE) * PLANE + spot, core)

    def piece(k):
        return pl.ds(pl.multiple_of(k * CHUNK, CHUNK), CHUNK)

    def load_own(k):
        return pltpu.make_async_copy(basis.at[:, piece(k)], own.at[:, piece(k)], load_sem.at[k])

    def load_adj(k):
        return pltpu.make_async_copy(adjoint.at[:, piece(k)], adj.at[:, piece(k)], adj_sem.at[k])

    def remote(src, dst, send_sem, recv_sem, device):
        return pltpu.make_async_remote_copy(
            src_ref=src, dst_ref=dst, send_sem=send_sem, recv_sem=recv_sem,
            device_id=device, device_id_type=MESH,
        )

    barrier = pltpu.get_barrier_semaphore()
    friends = [pair]
    friends += [plane_peer(step) for step in range(1, PLANE)]
    friends += [level_peer(step) for step in range(1, SIDE)]
    for friend in friends:
        pl.semaphore_signal(barrier, inc=1, device_id=friend, device_id_type=MESH)
    snap_rows = pl.ds(pl.multiple_of(core * half, half), half)
    load_snap = pltpu.make_async_copy(snaps, snap.at[snap_rows], small_sem.at[0])
    load_snap.start()
    for k in range(chunks):
        load_own(k).start()
        load_adj(k).start()
    root[...] = jnp.sqrt(volumes[...] * (1.0 / cells))
    acc[...] = jnp.zeros_like(acc)
    acc_snap[...] = jnp.zeros_like(acc_snap)

    pl.semaphore_wait(barrier, len(friends))
    send_snap = remote(snaps, snap.at[snap_rows], ss_sem.at[0], ss_sem.at[1], pair)
    send_snap.start()

    def send_own(k):
        return remote(basis.at[:, piece(k)], other.at[:, piece(k)], bs_sem.at[k], br_sem.at[k], pair)

    for k in range(chunks):
        send_own(k).start()

    def prepare(k, carry):
        cols = piece(k)
        load_own(k).wait()
        left_hi[:tile, cols], left_lo[:tile, cols] = split(own[:, cols] * root[:, cols])
        load_adj(k).wait()
        adj_hi[:, cols], adj_lo[:, cols] = split(adj[:, cols] * root[:, cols])
        return carry

    lax.fori_loop(0, chunks, prepare, 0)
    load_snap.wait()
    send_snap.wait()
    save_snap = pltpu.make_async_copy(snap, snaps_out, out_sem.at[0])
    save_snap.start()
    left_hi[tile:near], left_lo[tile:near] = split(snap[...] * root[...])

    def multiply(k, carry):
        cols = piece(k)
        send_own(k).wait_recv()
        pltpu.make_async_copy(other.at[:, cols], other_out.at[:, cols], out_sem.at[k + 1]).start()
        left_hi[near:, cols], left_lo[near:, cols] = split(other[:, cols] * root[:, cols])
        right = tuple(
            jnp.concatenate([a[:tile, cols], b[:, cols]], axis=0)
            for a, b in ((left_hi, adj_hi), (left_lo, adj_lo))
        )
        acc[...] += dot3((left_hi[:, cols], left_lo[:, cols]), right)
        both = (left_hi[tile:near, cols], left_lo[tile:near, cols])
        acc_snap[...] += dot3(both, both)
        return carry

    lax.fori_loop(0, chunks, multiply, 0)

    mid = tile // 2
    flat = share.shape[1]

    def put(row, value):
        for start in range(0, value.shape[0], flat):
            share[(row + start) // flat] = value[start : start + flat]

    put(0, jnp.concatenate([acc[:mid, :mid], acc[mid:tile, mid:tile]], axis=1))
    snap_square = jnp.concatenate(
        [0.5 * acc_snap[...], jnp.zeros((mid - snap_count, snap_count), f32)], axis=0
    )
    put(
        mid,
        jnp.concatenate(
            [acc[mid:tile, :mid], snap_square, jnp.zeros((mid, mid - snap_count), f32)], axis=1
        ),
    )
    mixed = acc[near:, :tile]
    put(tile, jnp.where(core == 0, mixed[:mid], mixed.T[mid:]))
    put(tile + mid, acc[tile:near, :tile])
    put(tile + mid + snap_count, acc[:tile, tile:])
    put(2 * tile + mid + snap_count, acc[near:, tile:])
    put(3 * tile + mid + snap_count, acc[tile:near, tile:])

    copies = [
        remote(share.at[in_plane(step)], slots.at[step], rs_sem.at[step], rr_sem.at[step],
               plane_peer(step))
        for step in range(1, PLANE)
    ]
    for copy in copies:
        copy.start()
    slots[0] = share[spot]
    for copy in copies:
        copy.wait_recv()
    value = slots[: PLANE // 2] + slots[PLANE // 2 :]
    value = value[: PLANE // 4] + value[PLANE // 4 :]
    value = value[: PLANE // 8] + value[PLANE // 8 :]
    part[0] = value[0] + value[1]

    z_copies = [
        remote(part.at[0], z_slots.at[step], zs_sem.at[step], zr_sem.at[step], level_peer(step))
        for step in range(1, SIDE)
    ]
    for copy in z_copies:
        copy.start()
    for copy in z_copies:
        copy.wait_recv()
    part[1] = (part[0] + z_slots[2]) + (z_slots[1] + z_slots[3])

    g_copies = [
        remote(part.at[1], total.at[0, spot], gs_sem.at[step], gr_sem.at[step], plane_peer(step))
        for step in range(1, PLANE)
    ]
    for copy in g_copies:
        copy.start()
    f_copies = [remote(part.at[1], total.at[1, spot], fs_sem.at[0], fr_sem.at[0], pair)]
    f_copies[0].start()
    total[0, spot] = part[1]
    for step in range(1, PLANE):
        source = in_plane(PLANE - step)
        remote(part.at[1], total.at[0, source], gs_sem.at[step], gr_sem.at[step], pair).wait_recv()
        f_copies.append(
            remote(total.at[0, source], total.at[1, source], fs_sem.at[step], fr_sem.at[step], pair)
        )
        f_copies[-1].start()
    for copy in f_copies:
        copy.wait()
    total_out[...] = total[...]
    for copy in copies + z_copies + g_copies:
        copy.wait_send()

    def finish(k, carry):
        send_own(k).wait_send()
        pltpu.make_async_copy(other.at[:, piece(k)], other_out.at[:, piece(k)], out_sem.at[k + 1]).wait()
        return carry

    lax.fori_loop(0, chunks, finish, 0)
    save_snap.wait()


def gather(cells, basis, adjoint, snapshots, volumes):
    tile, width = basis.shape
    snap_count = 2 * snapshots.shape[0]
    rows = 2 * tile + snap_count
    flat = (7 * tile // 2 + 2 * snap_count) // PLANE
    chunks = width // CHUNK
    dma = pltpu.SemaphoreType.DMA
    vmem = pltpu.VMEM
    any_spec = pl.BlockSpec(memory_space=pl.ANY)
    vmem_spec = pl.BlockSpec(memory_space=vmem)
    return pl.pallas_call(
        functools.partial(gather_kernel, cells),
        out_shape=(
            jax.ShapeDtypeStruct((tile, width), f32),
            jax.ShapeDtypeStruct((snap_count, width), f32),
            jax.ShapeDtypeStruct((2, PLANE, flat, tile), f32),
        ),
        in_specs=[any_spec, any_spec, any_spec, vmem_spec],
        out_specs=(any_spec, any_spec, vmem_spec),
        scratch_shapes=[
            vmem((tile, width), f32),
            vmem((tile, width), f32),
            vmem((tile, width), f32),
            vmem((snap_count, width), f32),
            vmem((1, width), f32),
            vmem((rows, width), bf16),
            vmem((rows, width), bf16),
            vmem((tile, width), bf16),
            vmem((tile, width), bf16),
            vmem((rows, 2 * tile), f32),
            vmem((snap_count, snap_count), f32),
            vmem((PLANE, flat, tile), f32),
            vmem((PLANE, flat, tile), f32),
            vmem((2, flat, tile), f32),
            vmem((SIDE, flat, tile), f32),
            vmem((2, PLANE, flat, tile), f32),
            dma((chunks,)),
            dma((chunks,)),
            dma((1,)),
            dma((chunks,)),
            dma((chunks,)),
            dma((2,)),
            dma((chunks + 1,)),
            dma((PLANE,)),
            dma((PLANE,)),
            dma((SIDE,)),
            dma((SIDE,)),
            dma((PLANE,)),
            dma((PLANE,)),
            dma((PLANE,)),
            dma((PLANE,)),
        ],
        compiler_params=pltpu.CompilerParams(
            collective_id=0, has_side_effects=True, vmem_limit_bytes=56 * 1024 * 1024
        ),
    )(basis, adjoint, snapshots, volumes)


def dot_nn(left, right):
    return lax.dot_general(left, right, (((1,), (0,)), ((), ())), preferred_element_type=f32)


def dot3_nn(left, right):
    rows = left[0].shape[0]
    both = dot_nn(jnp.concatenate([left[0], left[1]], axis=0), right[0])
    return both[:rows] + (dot_nn(left[0], right[1]) + both[rows:])


def exact_tn(left, right):
    return lax.dot_general(
        left, right, (((0,), (0,)), ((), ())), precision=highest, preferred_element_type=f32
    )


def inverse_factor(block, group):
    size = block.shape[0]
    eye = (
        lax.broadcasted_iota(jnp.int32, (size, size), 0)
        == lax.broadcasted_iota(jnp.int32, (size, size), 1)
    ).astype(f32)
    left = jnp.concatenate([block, eye], axis=1)
    done = []
    for start in range(0, size, group):
        count = size - start
        row = lax.broadcasted_iota(jnp.int32, (count, 2 * size), 0)
        cols = [
            jnp.broadcast_to(left[:, start + t : start + t + 1], (count, 2 * size))
            for t in range(group)
        ]
        for t in range(group):
            pivot = cols[t][t : t + 1, :]
            factor = jnp.where(row > t, cols[t], 0.0) * (1.0 / pivot)
            for u in range(t + 1, group):
                cols[u] = cols[u] - factor * cols[u][t : t + 1, :]
            done.append(left[t : t + 1, :] * lax.rsqrt(pivot))
            left = left - factor * left[t : t + 1, :]
        left = left[group:]
    return jnp.concatenate(done, axis=0)[:, size:]


def rotate_kernel(
    basis, other, snaps, total, singular,
    new_out, singular_out, hankel_out,
    rows, result, lead, inverse, coef_hi, coef_lo, in_sem, out_sem,
):
    tile, width = result.shape
    modes = 2 * tile
    snap_count = snaps.shape[0]
    chunks = width // CHUNK
    core = lax.axis_index("mode")
    first_core = core == 0

    def piece(k):
        return pl.ds(pl.multiple_of(k * CHUNK, CHUNK), CHUNK)

    def loads(k):
        cols = piece(k)
        return (
            pltpu.make_async_copy(basis.at[:, cols], rows.at[:tile, cols], in_sem.at[0, k]),
            pltpu.make_async_copy(other.at[:, cols], rows.at[tile:modes, cols], in_sem.at[1, k]),
            pltpu.make_async_copy(snaps.at[:, cols], rows.at[modes:, cols], in_sem.at[2, k]),
        )

    for k in range(chunks):
        for copy in loads(k):
            copy.start()

    s = singular[...]
    s2 = s * s
    mid = tile // 2

    def get(which, row, count):
        flat = total.shape[2]
        first = row // flat
        return total[which, first : first + count // flat].reshape(count, tile)

    def both_cores(row, count):
        mine, others = get(0, row, count), get(1, row, count)
        return jnp.where(first_core, mine, others), jnp.where(first_core, others, mine)

    halves = both_cores(tile + mid, snap_count)
    project_t = jnp.concatenate(halves, axis=1)
    low_diagonal, low_corner = both_cores(0, mid), both_cores(mid, mid)
    snap_square = sum(value[:snap_count, mid : mid + snap_count] for value in low_corner)
    lower = jnp.concatenate(both_cores(tile, mid), axis=0)
    between = exact_nn(halves[1], lower)
    diagonal = jnp.zeros((snap_count, snap_count), f32)
    one_side = exact_nt(between, halves[0])
    for part, ends, corner in zip(halves, low_diagonal, low_corner):
        ahead, behind = part[:, :mid], part[:, mid:]
        diagonal += exact_nt(exact_nn(ahead, ends[:, :mid]), ahead)
        diagonal += exact_nt(exact_nn(behind, ends[:, mid:]), behind)
        one_side += exact_nt(exact_nn(behind, corner[:, :mid]), ahead)
    scaled_t = project_t * s2
    pad = jnp.zeros((tile - 2 * snap_count, modes), f32)
    turned = jnp.concatenate([project_t, scaled_t, pad], axis=0).T
    by_mode, by_mode_scaled = turned[:, :snap_count], turned[:, snap_count : 2 * snap_count]
    inner = (snap_square - exact_nt(project_t, project_t)) + (diagonal + (one_side + one_side.T))
    side = by_mode_scaled + exact_nn(by_mode, inner)
    side_and_project = jnp.concatenate([side, by_mode], axis=1)
    eye = lax.broadcasted_iota(jnp.int32, (modes, modes), 0) == lax.broadcasted_iota(
        jnp.int32, (modes, modes), 1
    )
    lead[...] = jnp.where(eye, s2 * s2, 0.0) + exact_nt(
        side_and_project, turned[:, : 2 * snap_count]
    )
    inverse[...] = eye.astype(f32)
    size = 64
    for start in range(0, modes, size):
        stop = start + size
        small = inverse_factor(lead[start:stop, start:stop], 8)
        part = exact_nn(small, inverse[start:stop, :])
        inverse[start:stop, :] = part
        if stop < modes:
            upper = exact_nn(small, lead[start:stop, :])
            later = upper[:, stop:]
            lead[stop:, :] -= exact_tn(later, upper)
            inverse[stop:, :] -= exact_tn(later, part)

    mine = inverse[pl.ds(pl.multiple_of(core * tile, tile), tile), :]
    both = exact_nn(mine, side_and_project)
    on_snaps = both[:, snap_count:]
    on_modes = mine * s2
    image = (on_modes + exact_nn(on_snaps, project_t)) * s
    energy = exact_nt(jnp.ones((8, modes), f32), image * image) + exact_nt(
        jnp.ones((8, snap_count), f32), both[:, :snap_count] * both[:, :snap_count]
    )
    singular_out[...] = jnp.sqrt(energy[:1])

    on_first, on_second = on_modes[:, :tile], on_modes[:, tile:]
    coef = split(
        jnp.concatenate(
            [
                jnp.where(first_core, on_first, on_second),
                jnp.where(first_core, on_second, on_first),
                on_snaps,
            ],
            axis=1,
        )
    )
    coef_hi[...], coef_lo[...] = coef

    def rotate(k, carry):
        for copy in loads(k):
            copy.wait()
        cols = piece(k)
        result[:, cols] = dot3_nn((coef_hi[...], coef_lo[...]), split(rows[:, cols]))
        pltpu.make_async_copy(result.at[:, cols], new_out.at[:, cols], out_sem.at[k]).start()
        return carry

    lax.fori_loop(0, chunks, rotate, 0)

    base = tile + mid + snap_count
    swapped = (get(1, base + tile, tile), get(1, base, tile), get(1, base + modes, snap_count))
    straight = (get(0, base, tile), get(0, base + tile, tile), get(0, base + modes, snap_count))
    columns = jnp.concatenate(
        [
            jnp.concatenate(
                [jnp.where(first_core, a, b), jnp.where(first_core, b, a)], axis=1
            )
            for a, b in zip(straight, swapped)
        ],
        axis=0,
    )
    hankel_out[...] = dot3_nn(coef, split(columns))

    def finish(k, carry):
        pltpu.make_async_copy(result.at[:, piece(k)], new_out.at[:, piece(k)], out_sem.at[k]).wait()
        return carry

    lax.fori_loop(0, chunks, finish, 0)


def rotate(basis, other, snaps, total, singular):
    tile, width = basis.shape
    modes, snap_count = 2 * tile, snaps.shape[0]
    chunks = width // CHUNK
    dma = pltpu.SemaphoreType.DMA
    vmem = pltpu.VMEM
    any_spec = pl.BlockSpec(memory_space=pl.ANY)
    vmem_spec = pl.BlockSpec(memory_space=vmem)
    return pl.pallas_call(
        rotate_kernel,
        out_shape=(
            jax.ShapeDtypeStruct((tile, width), f32),
            jax.ShapeDtypeStruct((1, tile), f32),
            jax.ShapeDtypeStruct((tile, modes), f32),
        ),
        in_specs=[any_spec] * 3 + [vmem_spec] * 2,
        out_specs=(any_spec, vmem_spec, vmem_spec),
        scratch_shapes=[
            vmem((modes + snap_count, width), f32),
            vmem((tile, width), f32),
            vmem((modes, modes), f32),
            vmem((modes, modes), f32),
            vmem((tile, modes + snap_count), bf16),
            vmem((tile, modes + snap_count), bf16),
            dma((3, chunks)),
            dma((chunks,)),
        ],
        compiler_params=pltpu.CompilerParams(vmem_limit_bytes=56 * 1024 * 1024),
    )(basis, other, snaps, total, singular)


def shards(basis, adjoint, snapshots, volumes, singular):
    tile, width = basis.shape
    cells = float(width * lax.axis_size("space"))
    other, snaps, total = gather(
        cells, basis, adjoint, snapshots, volumes.reshape(1, width)
    )
    new_tile, new_singular, hankel = rotate(
        basis, other, snaps, total, singular.reshape(1, 2 * tile)
    )
    return new_tile, new_singular.reshape(tile), hankel


def solution(mesh):
    return jax.shard_map(
        shards,
        mesh=mesh,
        in_specs=(P("mode", "space"), P("mode", "space"), P("mode", "space"), P("space"), P()),
        out_specs=(P("mode", "space"), P("mode"), P("mode", None)),
        check_vma=False,
    )
```

```python
import functools

import jax
import jax.numpy as jnp
from jax import lax
from jax.experimental import pallas as pl
from jax.experimental.pallas import tpu as pltpu
from jax.sharding import PartitionSpec as P

MESH = pl.DeviceIdType.MESH
highest = lax.Precision.HIGHEST
f32 = jnp.float32
bf16 = jnp.bfloat16
SIDE = 4
PLANE = SIDE * SIDE
CHUNK = 1024


def split(value):
    high = value.astype(bf16)
    return high, (value - high.astype(f32)).astype(bf16)


def dot_nt(left, right):
    return lax.dot_general(left, right, (((1,), (1,)), ((), ())), preferred_element_type=f32)


def dot3(left, right):
    return dot_nt(left[0], right[0]) + (dot_nt(left[0], right[1]) + dot_nt(left[1], right[0]))


def exact_nt(left, right):
    return lax.dot_general(
        left, right, (((1,), (1,)), ((), ())), precision=highest, preferred_element_type=f32
    )


def exact_nn(left, right):
    return lax.dot_general(
        left, right, (((1,), (0,)), ((), ())), precision=highest, preferred_element_type=f32
    )


def dot_nn(left, right):
    return lax.dot_general(left, right, (((1,), (0,)), ((), ())), preferred_element_type=f32)


def dot3_nn(left, right):
    rows = left[0].shape[0]
    both = dot_nn(jnp.concatenate([left[0], left[1]], axis=0), right[0])
    return both[:rows] + (dot_nn(left[0], right[1]) + both[rows:])


def exact_tn(left, right):
    return lax.dot_general(
        left, right, (((0,), (0,)), ((), ())), precision=highest, preferred_element_type=f32
    )


def inverse_factor(block, group):
    size = block.shape[0]
    eye = (
        lax.broadcasted_iota(jnp.int32, (size, size), 0)
        == lax.broadcasted_iota(jnp.int32, (size, size), 1)
    ).astype(f32)
    left = jnp.concatenate([block, eye], axis=1)
    done = []
    for start in range(0, size, group):
        count = size - start
        row = lax.broadcasted_iota(jnp.int32, (count, 2 * size), 0)
        cols = [
            jnp.broadcast_to(left[:, start + t : start + t + 1], (count, 2 * size))
            for t in range(group)
        ]
        for t in range(group):
            pivot = cols[t][t : t + 1, :]
            factor = jnp.where(row > t, cols[t], 0.0) * (1.0 / pivot)
            for u in range(t + 1, group):
                cols[u] = cols[u] - factor * cols[u][t : t + 1, :]
            done.append(left[t : t + 1, :] * lax.rsqrt(pivot))
            left = left - factor * left[t : t + 1, :]
        left = left[group:]
    return jnp.concatenate(done, axis=0)[:, size:]


def factor_kernel(
    cells,
    basis, adjoint, snaps, volumes, singular,
    other_out, snaps_out, coef_out, singular_out, hankel_out,
    own, other, adj, snap, root,
    left_hi, left_lo, adj_hi, adj_lo,
    acc, acc_cross, acc_snap, lead, inverse,
    g_share, g_slots, g_part, g_level, g_total,
    h_share, h_slots, h_part, h_level, h_total,
    load_sem, adj_sem, small_sem, bs_sem, br_sem, ss_sem, out_sem,
    rs_sem, rr_sem, zs_sem, zr_sem, gs_sem, gr_sem, fs_sem, fr_sem,
):
    tile, width = own.shape
    modes = 2 * tile
    mid, low = tile // 2, tile // 4
    snap_count = snap.shape[0]
    half = snap_count // 2
    chunks = width // CHUNK
    near = tile + snap_count
    place = lax.axis_index("space")
    core = lax.axis_index("mode")
    first_core = core == 0
    pair = (place, 1 - core)
    spot = lax.rem(place, PLANE)
    level = place // PLANE

    def in_plane(step):
        return lax.rem(spot + step, PLANE)

    def plane_peer(step):
        return (level * PLANE + in_plane(step), core)

    def level_peer(step):
        return (lax.rem(level + step, SIDE) * PLANE + spot, core)

    def piece(k):
        return pl.ds(pl.multiple_of(k * CHUNK, CHUNK), CHUNK)

    def load_own(k):
        return pltpu.make_async_copy(basis.at[:, piece(k)], own.at[:, piece(k)], load_sem.at[k])

    def load_adj(k):
        return pltpu.make_async_copy(adjoint.at[:, piece(k)], adj.at[:, piece(k)], adj_sem.at[k])

    def remote(src, dst, send_sem, recv_sem, device):
        return pltpu.make_async_remote_copy(
            src_ref=src, dst_ref=dst, send_sem=send_sem, recv_sem=recv_sem,
            device_id=device, device_id_type=MESH,
        )

    barrier = pltpu.get_barrier_semaphore()
    friends = [pair]
    friends += [plane_peer(step) for step in range(1, PLANE)]
    friends += [level_peer(step) for step in range(1, SIDE)]
    for friend in friends:
        pl.semaphore_signal(barrier, inc=1, device_id=friend, device_id_type=MESH)
    snap_rows = pl.ds(pl.multiple_of(core * half, half), half)
    load_snap = pltpu.make_async_copy(snaps, snap.at[snap_rows], small_sem.at[0])
    load_snap.start()
    for k in range(chunks):
        load_own(k).start()
    for k in range(chunks):
        load_adj(k).start()
    root[...] = jnp.sqrt(volumes[...] * (1.0 / cells))
    for ref in (acc, acc_cross, acc_snap, h_share):
        ref[...] = jnp.zeros_like(ref)

    pl.semaphore_wait(barrier, len(friends))
    send_snap = remote(snaps, snap.at[snap_rows], ss_sem.at[0], ss_sem.at[1], pair)
    send_snap.start()

    def send_own(k):
        return remote(basis.at[:, piece(k)], other.at[:, piece(k)], bs_sem.at[k], br_sem.at[k], pair)

    def turn(k, which):
        return lax.rem(k + which * (chunks // 2), chunks)

    for k in range(chunks):
        send_own(turn(k, 1 - core)).start()

    def prepare(k, carry):
        cols = piece(k)
        load_own(k).wait()
        left_hi[:tile, cols], left_lo[:tile, cols] = split(own[:, cols] * root[:, cols])
        return carry

    lax.fori_loop(0, chunks, prepare, 0)
    load_snap.wait()
    send_snap.wait()
    save_snap = pltpu.make_async_copy(snap, snaps_out, out_sem.at[0])
    save_snap.start()
    left_hi[tile:near], left_lo[tile:near] = split(snap[...] * root[...])

    def multiply_own(k, carry):
        cols = piece(k)
        right = (left_hi[:tile, cols], left_lo[:tile, cols])
        acc[:near] += dot3((left_hi[:near, cols], left_lo[:near, cols]), right)
        both = (left_hi[tile:near, cols], left_lo[tile:near, cols])
        acc_snap[...] += dot3(both, both)
        return carry

    lax.fori_loop(0, chunks, multiply_own, 0)

    def arrive(k):
        cols = piece(k)
        send_own(k).wait_recv()
        pltpu.make_async_copy(other.at[:, cols], other_out.at[:, cols], out_sem.at[k + 1]).start()
        left_hi[near:, cols], left_lo[near:, cols] = split(other[:, cols] * root[:, cols])
        return cols

    def multiply_other(step, carry):
        cols = arrive(turn(step, core))
        acc[near:] += dot3(
            (left_hi[near:, cols], left_lo[near:, cols]), (left_hi[:tile, cols], left_lo[:tile, cols])
        )
        return carry

    lax.fori_loop(0, chunks // 2, multiply_other, 0)

    def put(row, value):
        flat = g_share.shape[1]
        for start in range(0, value.shape[0], flat):
            g_share[(row + start) // flat] = value[start : start + flat]

    ahead = jnp.concatenate(
        [jnp.concatenate([acc[:low, :low], 0.5 * acc_snap[...]], axis=1), acc[low:mid, :mid]], axis=0
    )
    put(0, jnp.concatenate([ahead, acc[mid:tile, mid:tile]], axis=1))
    by_snap = acc[tile:near, :tile]
    put(
        mid,
        jnp.concatenate(
            [acc[mid:tile, :mid], jnp.concatenate([by_snap[:, :mid], by_snap[:, mid:]], axis=0)], axis=1
        ),
    )
    mixed = acc[near:, :]
    put(tile, jnp.where(first_core, mixed, mixed.T))

    def scatter(group, share, slots):
        copies = [
            remote(share.at[in_plane(step)], slots.at[step], rs_sem.at[group, step],
                   rr_sem.at[group, step], plane_peer(step))
            for step in range(1, PLANE)
        ]
        for copy in copies:
            copy.start()
        slots[0] = share[spot]
        return copies

    def exchange(group, copies, slots, part, levels):
        for copy in copies:
            copy.wait()
        value = slots[: PLANE // 2] + slots[PLANE // 2 :]
        value = value[: PLANE // 4] + value[PLANE // 4 :]
        value = value[: PLANE // 8] + value[PLANE // 8 :]
        part[0] = value[0] + value[1]
        copies = [
            remote(part.at[0], levels.at[step], zs_sem.at[group, step], zr_sem.at[group, step],
                   level_peer(step))
            for step in range(1, SIDE)
        ]
        for copy in copies:
            copy.start()
        return copies

    def spread(group, copies, part, levels, total):
        for copy in copies:
            copy.wait()
        part[1] = (part[0] + levels[2]) + (levels[1] + levels[3])
        copies = [
            remote(part.at[1], total.at[0, spot], gs_sem.at[group, step], gr_sem.at[group, step],
                   plane_peer(step))
            for step in range(1, PLANE)
        ]
        passed = [remote(part.at[1], total.at[1, spot], fs_sem.at[group, 0], fr_sem.at[group, 0], pair)]
        for copy in copies + passed:
            copy.start()
        total[0, spot] = part[1]
        return copies, passed

    def pass_on(group, copies, passed, part, total):
        for step in range(1, PLANE):
            source = in_plane(PLANE - step)
            remote(part.at[1], total.at[0, source], gs_sem.at[group, step], gr_sem.at[group, step],
                   pair).wait_recv()
            passed.append(
                remote(total.at[0, source], total.at[1, source], fs_sem.at[group, step],
                       fr_sem.at[group, step], pair)
            )
            passed[-1].start()
        for copy in copies:
            copy.wait_send()
        return passed

    copies = scatter(0, g_share, g_slots)

    def adjoint_own(k, carry):
        cols = piece(k)
        load_adj(k).wait()
        right = split(adj[:, cols] * root[:, cols])
        adj_hi[:, cols], adj_lo[:, cols] = right
        acc_cross[:near] += dot3((left_hi[:near, cols], left_lo[:near, cols]), right)
        return carry

    def adjoint_other(k, carry):
        cols = piece(k)
        acc_cross[near:] += dot3(
            (left_hi[near:, cols], left_lo[near:, cols]), (adj_hi[:, cols], adj_lo[:, cols])
        )
        return carry

    def rest(step, carry):
        arrive(turn(step, core))
        return carry

    lax.fori_loop(0, chunks, adjoint_own, 0)
    copies = exchange(0, copies, g_slots, g_part, g_level)
    lax.fori_loop(chunks // 2, chunks, rest, 0)
    lax.fori_loop(0, chunks, adjoint_other, 0)
    copies, passed = spread(0, copies, g_part, g_level, g_total)
    flat = h_share.shape[1]
    count = (modes + snap_count) // flat
    h_share[:count] = acc_cross[...].reshape(count, flat, tile)
    h_copies = scatter(1, h_share, h_slots)
    for copy in pass_on(0, copies, passed, g_part, g_total):
        copy.wait()

    def get(which, row, rows):
        size = g_total.shape[2]
        return g_total[which, row // size : (row + rows) // size].reshape(rows, tile)

    def by_core(mine, others):
        return jnp.where(first_core, mine, others), jnp.where(first_core, others, mine)

    s = singular[...]
    s2 = s * s
    tops = by_core(get(0, 0, mid), get(1, 0, mid))
    bottoms = by_core(get(0, mid, mid), get(1, mid, mid))
    lower = get(0, tile, tile) + get(1, tile, tile)
    halves = [
        jnp.concatenate([value[:low, mid:], value[low:, mid:]], axis=1) for value in bottoms
    ]
    project_t = jnp.concatenate(halves, axis=1)
    snap_square = tops[0][:low, low:mid] + tops[1][:low, low:mid]
    one_side = exact_nt(exact_nn(halves[1], lower), halves[0])
    diagonal = snap_square - exact_nt(project_t, project_t)
    for part, top, bottom in zip(halves, tops, bottoms):
        ahead, behind = part[:, :mid], part[:, mid:]
        ends = jnp.concatenate(
            [jnp.concatenate([top[:low, :low], top[low:, :low].T], axis=1), top[low:, :mid]], axis=0
        )
        diagonal += exact_nt(exact_nn(ahead, ends), ahead)
        diagonal += exact_nt(exact_nn(behind, top[:, mid:]), behind)
        one_side += exact_nt(exact_nn(behind, bottom[:, :mid]), ahead)
    inner = diagonal + (one_side + one_side.T)

    pad = jnp.zeros((tile - 2 * snap_count, modes), f32)
    turned = jnp.concatenate([project_t, project_t * s2, pad], axis=0).T
    by_mode, by_mode_scaled = turned[:, :snap_count], turned[:, snap_count : 2 * snap_count]
    side = by_mode_scaled + exact_nn(by_mode, inner)
    side_and_project = jnp.concatenate([side, by_mode], axis=1)
    eye = lax.broadcasted_iota(jnp.int32, (modes, modes), 0) == lax.broadcasted_iota(
        jnp.int32, (modes, modes), 1
    )
    lead[...] = jnp.where(eye, s2 * s2, 0.0) + exact_nt(
        side_and_project, turned[:, : 2 * snap_count]
    )
    inverse[...] = eye.astype(f32)
    size = 64
    for start in range(0, modes, size):
        stop = start + size
        small = inverse_factor(lead[start:stop, start:stop], 8)
        part = exact_nn(small, inverse[start:stop, :])
        inverse[start:stop, :] = part
        if stop < modes:
            upper = exact_nn(small, lead[start:stop, :])
            later = upper[:, stop:]
            lead[stop:, :] -= exact_tn(later, upper)
            inverse[stop:, :] -= exact_tn(later, part)
        if start == 0:
            h_copies = exchange(1, h_copies, h_slots, h_part, h_level)
        elif start == size:
            h_copies, h_passed = spread(1, h_copies, h_part, h_level, h_total)
        elif start == 2 * size:
            h_passed = pass_on(1, h_copies, h_passed, h_part, h_total)

    mine = inverse[pl.ds(pl.multiple_of(core * tile, tile), tile), :]
    both = exact_nn(mine, side_and_project)
    on_snaps = both[:, snap_count:]
    on_modes = mine * s2
    image = (on_modes + exact_nn(on_snaps, project_t)) * s
    energy = exact_nt(jnp.ones((8, modes), f32), image * image) + exact_nt(
        jnp.ones((8, snap_count), f32), both[:, :snap_count] * both[:, :snap_count]
    )
    singular_out[...] = jnp.sqrt(energy[:1])
    on_own, on_other = by_core(on_modes[:, :tile], on_modes[:, tile:])
    coef = jnp.concatenate([on_own, on_other, on_snaps], axis=1)
    coef_out[...] = coef

    for copy in h_passed:
        copy.wait()
    straight = h_total[0, :count].reshape(count * flat, tile)
    swapped = h_total[1, :count].reshape(count * flat, tile)
    swapped = jnp.concatenate([swapped[near:], swapped[tile:near], swapped[:tile]], axis=0)
    columns = jnp.concatenate(by_core(straight, swapped), axis=1)
    columns = jnp.concatenate([columns[:tile], columns[near:], columns[tile:near]], axis=0)
    hankel_out[...] = dot3_nn(split(coef), split(columns))

    def finish(k, carry):
        send_own(k).wait_send()
        pltpu.make_async_copy(other.at[:, piece(k)], other_out.at[:, piece(k)], out_sem.at[k + 1]).wait()
        return carry

    lax.fori_loop(0, chunks, finish, 0)
    save_snap.wait()


def factor(cells, basis, adjoint, snapshots, volumes, singular):
    tile, width = basis.shape
    snap_count = 2 * snapshots.shape[0]
    modes = 2 * tile
    rows = modes + snap_count
    chunks = width // CHUNK
    dma = pltpu.SemaphoreType.DMA
    vmem = pltpu.VMEM
    any_spec = pl.BlockSpec(memory_space=pl.ANY)
    vmem_spec = pl.BlockSpec(memory_space=vmem)

    def sums(flat):
        return [
            vmem((PLANE, flat, tile), f32),
            vmem((PLANE, flat, tile), f32),
            vmem((2, flat, tile), f32),
            vmem((SIDE, flat, tile), f32),
            vmem((2, PLANE, flat, tile), f32),
        ]

    return pl.pallas_call(
        functools.partial(factor_kernel, cells),
        out_shape=(
            jax.ShapeDtypeStruct((tile, width), f32),
            jax.ShapeDtypeStruct((snap_count, width), f32),
            jax.ShapeDtypeStruct((tile, rows), f32),
            jax.ShapeDtypeStruct((1, tile), f32),
            jax.ShapeDtypeStruct((tile, modes), f32),
        ),
        in_specs=[any_spec, any_spec, any_spec, vmem_spec, vmem_spec],
        out_specs=(any_spec, any_spec, vmem_spec, vmem_spec, vmem_spec),
        scratch_shapes=[
            vmem((tile, width), f32),
            vmem((tile, width), f32),
            vmem((tile, width), f32),
            vmem((snap_count, width), f32),
            vmem((1, width), f32),
            vmem((rows, width), bf16),
            vmem((rows, width), bf16),
            vmem((tile, width), bf16),
            vmem((tile, width), bf16),
            vmem((rows, tile), f32),
            vmem((rows, tile), f32),
            vmem((snap_count, snap_count), f32),
            vmem((modes, modes), f32),
            vmem((modes, modes), f32),
            *sums(16),
            *sums(24),
            dma((chunks,)),
            dma((chunks,)),
            dma((1,)),
            dma((chunks,)),
            dma((chunks,)),
            dma((2,)),
            dma((chunks + 1,)),
            dma((2, PLANE)),
            dma((2, PLANE)),
            dma((2, SIDE)),
            dma((2, SIDE)),
            dma((2, PLANE)),
            dma((2, PLANE)),
            dma((2, PLANE)),
            dma((2, PLANE)),
        ],
        compiler_params=pltpu.CompilerParams(
            collective_id=0, has_side_effects=True, vmem_limit_bytes=56 * 1024 * 1024
        ),
    )(basis, adjoint, snapshots, volumes, singular)


def rotate_kernel(basis, other, snaps, coef, new_out, rows, result, in_sem, out_sem):
    tile, width = result.shape
    modes = 2 * tile
    chunks = width // CHUNK

    def piece(k):
        return pl.ds(pl.multiple_of(k * CHUNK, CHUNK), CHUNK)

    def loads(k):
        cols = piece(k)
        return (
            pltpu.make_async_copy(basis.at[:, cols], rows.at[:tile, cols], in_sem.at[0, k]),
            pltpu.make_async_copy(other.at[:, cols], rows.at[tile:modes, cols], in_sem.at[1, k]),
            pltpu.make_async_copy(snaps.at[:, cols], rows.at[modes:, cols], in_sem.at[2, k]),
        )

    for k in range(chunks):
        for copy in loads(k):
            copy.start()
    parts = split(coef[...])

    def step(k, carry):
        for copy in loads(k):
            copy.wait()
        cols = piece(k)
        result[:, cols] = dot3_nn(parts, split(rows[:, cols]))
        pltpu.make_async_copy(result.at[:, cols], new_out.at[:, cols], out_sem.at[k]).start()
        return carry

    lax.fori_loop(0, chunks, step, 0)

    def finish(k, carry):
        pltpu.make_async_copy(result.at[:, piece(k)], new_out.at[:, piece(k)], out_sem.at[k]).wait()
        return carry

    lax.fori_loop(0, chunks, finish, 0)


def rotate(basis, other, snaps, coef):
    tile, width = basis.shape
    chunks = width // CHUNK
    dma = pltpu.SemaphoreType.DMA
    any_spec = pl.BlockSpec(memory_space=pl.ANY)
    return pl.pallas_call(
        rotate_kernel,
        out_shape=jax.ShapeDtypeStruct((tile, width), f32),
        in_specs=[any_spec] * 3 + [pl.BlockSpec(memory_space=pltpu.VMEM)],
        out_specs=any_spec,
        scratch_shapes=[
            pltpu.VMEM((coef.shape[1], width), f32),
            pltpu.VMEM((tile, width), f32),
            dma((3, chunks)),
            dma((chunks,)),
        ],
        compiler_params=pltpu.CompilerParams(vmem_limit_bytes=56 * 1024 * 1024),
    )(basis, other, snaps, coef)


def shards(basis, adjoint, snapshots, volumes, singular):
    tile, width = basis.shape
    cells = float(width * lax.axis_size("space"))
    other, snaps, coef, new_singular, hankel = factor(
        cells, basis, adjoint, snapshots, volumes.reshape(1, width), singular.reshape(1, 2 * tile)
    )
    return rotate(basis, other, snaps, coef), new_singular.reshape(tile), hankel


def solution(mesh):
    return jax.shard_map(
        shards,
        mesh=mesh,
        in_specs=(P("mode", "space"), P("mode", "space"), P("mode", "space"), P("space"), P()),
        out_specs=(P("mode", "space"), P("mode"), P("mode", None)),
        check_vma=False,
    )
```

```python
import functools

import jax
import jax.numpy as jnp
from jax import lax
from jax.experimental import pallas as pl
from jax.experimental.pallas import tpu as pltpu
from jax.sharding import PartitionSpec as P

MESH = pl.DeviceIdType.MESH
highest = lax.Precision.HIGHEST
f32 = jnp.float32
bf16 = jnp.bfloat16
SIDE = 4
PLANE = SIDE * SIDE
CHUNK = 1024


def split(value):
    high = value.astype(bf16)
    return high, (value - high.astype(f32)).astype(bf16)


def dot_nt(left, right):
    return lax.dot_general(left, right, (((1,), (1,)), ((), ())), preferred_element_type=f32)


def dot3(left, right):
    return dot_nt(left[0], right[0]) + (dot_nt(left[0], right[1]) + dot_nt(left[1], right[0]))


def exact_nt(left, right):
    return lax.dot_general(
        left, right, (((1,), (1,)), ((), ())), precision=highest, preferred_element_type=f32
    )


def exact_nn(left, right):
    return lax.dot_general(
        left, right, (((1,), (0,)), ((), ())), precision=highest, preferred_element_type=f32
    )


def gather_kernel(
    cells,
    basis, adjoint, snaps, volumes,
    hi_out, lo_out, total_out,
    own, other, adj, snap, root,
    left_hi, left_lo, adj_hi, adj_lo,
    acc, acc_snap, share, slots, part, z_slots, total,
    load_sem, adj_sem, small_sem, bs_sem, br_sem, ss_sem, out_sem,
    rs_sem, rr_sem, zs_sem, zr_sem, gs_sem, gr_sem, fs_sem, fr_sem,
):
    tile, width = own.shape
    snap_count = snap.shape[0]
    half = snap_count // 2
    chunks = width // CHUNK
    near = tile + snap_count
    place = lax.axis_index("space")
    core = lax.axis_index("mode")
    pair = (place, 1 - core)
    spot = lax.rem(place, PLANE)
    level = place // PLANE

    def in_plane(step):
        return lax.rem(spot + step, PLANE)

    def plane_peer(step):
        return (level * PLANE + in_plane(step), core)

    def level_peer(step):
        return (lax.rem(level + step, SIDE) * PLANE + spot, core)

    def piece(k):
        return pl.ds(pl.multiple_of(k * CHUNK, CHUNK), CHUNK)

    def load_own(k):
        return pltpu.make_async_copy(basis.at[:, piece(k)], own.at[:, piece(k)], load_sem.at[k])

    def load_adj(k):
        return pltpu.make_async_copy(adjoint.at[:, piece(k)], adj.at[:, piece(k)], adj_sem.at[k])

    def remote(src, dst, send_sem, recv_sem, device):
        return pltpu.make_async_remote_copy(
            src_ref=src, dst_ref=dst, send_sem=send_sem, recv_sem=recv_sem,
            device_id=device, device_id_type=MESH,
        )

    barrier = pltpu.get_barrier_semaphore()
    friends = [pair]
    friends += [plane_peer(step) for step in range(1, PLANE)]
    friends += [level_peer(step) for step in range(1, SIDE)]
    for friend in friends:
        pl.semaphore_signal(barrier, inc=1, device_id=friend, device_id_type=MESH)
    snap_rows = pl.ds(pl.multiple_of(core * half, half), half)
    load_snap = pltpu.make_async_copy(snaps, snap.at[snap_rows], small_sem.at[0])
    load_snap.start()
    for k in range(chunks):
        load_own(k).start()
        load_adj(k).start()
    root[...] = jnp.sqrt(volumes[...] * (1.0 / cells))
    acc[...] = jnp.zeros_like(acc)
    acc_snap[...] = jnp.zeros_like(acc_snap)

    pl.semaphore_wait(barrier, len(friends))
    send_snap = remote(snaps, snap.at[snap_rows], ss_sem.at[0], ss_sem.at[1], pair)
    send_snap.start()

    def send_own(k):
        return remote(basis.at[:, piece(k)], other.at[:, piece(k)], bs_sem.at[k], br_sem.at[k], pair)

    for k in range(chunks):
        send_own(k).start()

    def prepare(k, carry):
        cols = piece(k)
        load_own(k).wait()
        left_hi[:tile, cols], left_lo[:tile, cols] = split(own[:, cols] * root[:, cols])
        load_adj(k).wait()
        adj_hi[:, cols], adj_lo[:, cols] = split(adj[:, cols] * root[:, cols])
        return carry

    lax.fori_loop(0, chunks, prepare, 0)
    load_snap.wait()
    send_snap.wait()
    left_hi[tile:near], left_lo[tile:near] = split(snap[...] * root[...])

    def saves(k):
        cols = piece(k)
        return (
            pltpu.make_async_copy(left_hi.at[:, cols], hi_out.at[:, cols], out_sem.at[0, k]),
            pltpu.make_async_copy(left_lo.at[:, cols], lo_out.at[:, cols], out_sem.at[1, k]),
        )

    def multiply(k, carry):
        cols = piece(k)
        send_own(k).wait_recv()
        left_hi[near:, cols], left_lo[near:, cols] = split(other[:, cols] * root[:, cols])
        for copy in saves(k):
            copy.start()
        right = tuple(
            jnp.concatenate([a[:tile, cols], b[:, cols]], axis=0)
            for a, b in ((left_hi, adj_hi), (left_lo, adj_lo))
        )
        acc[...] += dot3((left_hi[:, cols], left_lo[:, cols]), right)
        both = (left_hi[tile:near, cols], left_lo[tile:near, cols])
        acc_snap[...] += dot3(both, both)
        return carry

    lax.fori_loop(0, chunks, multiply, 0)

    mid = tile // 2
    flat = share.shape[1]

    def put(row, value):
        for start in range(0, value.shape[0], flat):
            share[(row + start) // flat] = value[start : start + flat]

    put(0, jnp.concatenate([acc[:mid, :mid], acc[mid:tile, mid:tile]], axis=1))
    snap_square = jnp.concatenate(
        [0.5 * acc_snap[...], jnp.zeros((mid - snap_count, snap_count), f32)], axis=0
    )
    put(
        mid,
        jnp.concatenate(
            [acc[mid:tile, :mid], snap_square, jnp.zeros((mid, mid - snap_count), f32)], axis=1
        ),
    )
    mixed = acc[near:, :tile]
    put(tile, jnp.where(core == 0, mixed[:mid], mixed.T[mid:]))
    put(tile + mid, acc[tile:near, :tile])
    put(tile + mid + snap_count, acc[:tile, tile:])
    put(2 * tile + mid + snap_count, acc[near:, tile:])
    put(3 * tile + mid + snap_count, acc[tile:near, tile:])

    copies = [
        remote(share.at[in_plane(step)], slots.at[step], rs_sem.at[step], rr_sem.at[step],
               plane_peer(step))
        for step in range(1, PLANE)
    ]
    for copy in copies:
        copy.start()
    slots[0] = share[spot]
    for copy in copies:
        copy.wait_recv()
    value = slots[: PLANE // 2] + slots[PLANE // 2 :]
    value = value[: PLANE // 4] + value[PLANE // 4 :]
    value = value[: PLANE // 8] + value[PLANE // 8 :]
    part[0] = value[0] + value[1]

    z_copies = [
        remote(part.at[0], z_slots.at[step], zs_sem.at[step], zr_sem.at[step], level_peer(step))
        for step in range(1, SIDE)
    ]
    for copy in z_copies:
        copy.start()
    for copy in z_copies:
        copy.wait_recv()
    part[1] = (part[0] + z_slots[2]) + (z_slots[1] + z_slots[3])

    g_copies = [
        remote(part.at[1], total.at[0, spot], gs_sem.at[step], gr_sem.at[step], plane_peer(step))
        for step in range(1, PLANE)
    ]
    for copy in g_copies:
        copy.start()
    f_copies = [remote(part.at[1], total.at[1, spot], fs_sem.at[0], fr_sem.at[0], pair)]
    f_copies[0].start()
    total[0, spot] = part[1]
    for step in range(1, PLANE):
        source = in_plane(PLANE - step)
        remote(part.at[1], total.at[0, source], gs_sem.at[step], gr_sem.at[step], pair).wait_recv()
        f_copies.append(
            remote(total.at[0, source], total.at[1, source], fs_sem.at[step], fr_sem.at[step], pair)
        )
        f_copies[-1].start()
    for copy in f_copies:
        copy.wait()
    total_out[...] = total[...]
    for copy in copies + z_copies + g_copies:
        copy.wait_send()

    def finish(k, carry):
        send_own(k).wait_send()
        for copy in saves(k):
            copy.wait()
        return carry

    lax.fori_loop(0, chunks, finish, 0)


def gather(cells, basis, adjoint, snapshots, volumes):
    tile, width = basis.shape
    snap_count = 2 * snapshots.shape[0]
    rows = 2 * tile + snap_count
    flat = (7 * tile // 2 + 2 * snap_count) // PLANE
    chunks = width // CHUNK
    dma = pltpu.SemaphoreType.DMA
    vmem = pltpu.VMEM
    any_spec = pl.BlockSpec(memory_space=pl.ANY)
    vmem_spec = pl.BlockSpec(memory_space=vmem)
    return pl.pallas_call(
        functools.partial(gather_kernel, cells),
        out_shape=(
            jax.ShapeDtypeStruct((rows, width), bf16),
            jax.ShapeDtypeStruct((rows, width), bf16),
            jax.ShapeDtypeStruct((2, PLANE, flat, tile), f32),
        ),
        in_specs=[any_spec, any_spec, any_spec, vmem_spec],
        out_specs=(any_spec, any_spec, vmem_spec),
        scratch_shapes=[
            vmem((tile, width), f32),
            vmem((tile, width), f32),
            vmem((tile, width), f32),
            vmem((snap_count, width), f32),
            vmem((1, width), f32),
            vmem((rows, width), bf16),
            vmem((rows, width), bf16),
            vmem((tile, width), bf16),
            vmem((tile, width), bf16),
            vmem((rows, 2 * tile), f32),
            vmem((snap_count, snap_count), f32),
            vmem((PLANE, flat, tile), f32),
            vmem((PLANE, flat, tile), f32),
            vmem((2, flat, tile), f32),
            vmem((SIDE, flat, tile), f32),
            vmem((2, PLANE, flat, tile), f32),
            dma((chunks,)),
            dma((chunks,)),
            dma((1,)),
            dma((chunks,)),
            dma((chunks,)),
            dma((2,)),
            dma((2, chunks)),
            dma((PLANE,)),
            dma((PLANE,)),
            dma((SIDE,)),
            dma((SIDE,)),
            dma((PLANE,)),
            dma((PLANE,)),
            dma((PLANE,)),
            dma((PLANE,)),
        ],
        compiler_params=pltpu.CompilerParams(
            collective_id=0, has_side_effects=True, vmem_limit_bytes=56 * 1024 * 1024
        ),
    )(basis, adjoint, snapshots, volumes)


def dot_nn(left, right):
    return lax.dot_general(left, right, (((1,), (0,)), ((), ())), preferred_element_type=f32)


def dot3_nn(left, right):
    rows = left[0].shape[0]
    both = dot_nn(jnp.concatenate([left[0], left[1]], axis=0), right[0])
    return both[:rows] + (dot_nn(left[0], right[1]) + both[rows:])


def exact_tn(left, right):
    return lax.dot_general(
        left, right, (((0,), (0,)), ((), ())), precision=highest, preferred_element_type=f32
    )


def inverse_factors(blocks, group):
    size = blocks[0].shape[0]
    width = 2 * size
    eye = (
        lax.broadcasted_iota(jnp.int32, (size, size), 0)
        == lax.broadcasted_iota(jnp.int32, (size, size), 1)
    ).astype(f32)
    lefts = [jnp.concatenate([block, eye], axis=1) for block in blocks]
    done = [[] for _ in blocks]
    for start in range(0, size, group):
        count = size - start
        row = lax.broadcasted_iota(jnp.int32, (count, width), 0)
        cols = [
            [
                jnp.broadcast_to(left[:, start + t : start + t + 1], (count, width))
                for t in range(group)
            ]
            for left in lefts
        ]
        for t in range(group):
            for n, col in enumerate(cols):
                pivot = col[t][t : t + 1, :]
                factor = jnp.where(row > t, col[t], 0.0) * (1.0 / pivot)
                for u in range(t + 1, group):
                    col[u] = col[u] - factor * col[u][t : t + 1, :]
                done[n].append(lefts[n][t : t + 1, :] * lax.rsqrt(pivot))
                lefts[n] = lefts[n] - factor * lefts[n][t : t + 1, :]
        lefts = [left[group:] for left in lefts]
    return [jnp.concatenate(rows, axis=0)[:, size:] for rows in done]


def paired_inverses(blocks, group):
    size = blocks[0].shape[0]
    half, width = size // 2, 2 * size
    eye = (
        lax.broadcasted_iota(jnp.int32, (size, size), 0)
        == lax.broadcasted_iota(jnp.int32, (size, size), 1)
    ).astype(f32)
    lefts = [jnp.concatenate([block, eye], axis=1) for block in blocks]
    row = lax.broadcasted_iota(jnp.int32, (size, width), 0)
    row = jnp.where(row >= half, row - half, row)
    entries = [([], [], []) for _ in blocks]
    for start in range(0, half, group):
        places = list(range(start, start + group)) + list(range(half + start, half + start + group))
        cols = [
            [jnp.broadcast_to(left[:, at : at + 1], (size, width)) for at in places] for left in lefts
        ]
        for t in range(group):
            at = start + t
            upper, lower = slice(at, at + 1), slice(half + at, half + at + 1)
            below = row > at
            for n, col in enumerate(cols):
                first, second = col[t], col[group + t]
                alpha, beta, delta = first[upper], second[upper], second[lower]
                scale = 1.0 / (alpha * delta - beta * beta)
                a, b, c = delta * scale, -(beta * scale), alpha * scale
                for kept, value in zip(entries[n], (a, b, c)):
                    kept.append(value)
                on_upper = jnp.where(below, first * a + second * b, 0.0)
                on_lower = jnp.where(below, first * b + second * c, 0.0)
                for u in list(range(t + 1, group)) + list(range(group + t + 1, 2 * group)):
                    col[u] = col[u] - (on_upper * col[u][upper] + on_lower * col[u][lower])
                lefts[n] = lefts[n] - (on_upper * lefts[n][upper] + on_lower * lefts[n][lower])
    return [
        (left[:, size:], [jnp.concatenate(kept, axis=0) for kept in kinds])
        for left, kinds in zip(lefts, entries)
    ]


def own_inverse(project_t, s2, gram, first_core):
    snap_count, modes = project_t.shape
    tile, size = modes // 2, 64
    lane = lax.broadcasted_iota(jnp.int32, (1, modes), 1)
    offset = jnp.where(first_core, 0, tile)
    s4 = s2 * s2
    joined = jnp.concatenate([project_t * s2, project_t], axis=0)
    over2, over4 = project_t / s2, project_t / s4
    eye = (
        lax.broadcasted_iota(jnp.int32, (snap_count, snap_count), 0)
        == lax.broadcasted_iota(jnp.int32, (snap_count, snap_count), 1)
    ).astype(f32)
    diagonal = (
        lax.broadcasted_iota(jnp.int32, (tile, tile), 0)
        == lax.broadcasted_iota(jnp.int32, (tile, tile), 1)
    )
    own_s4 = jnp.where(first_core, s4[:, :tile], s4[:, tile:])
    own_diagonal = jnp.where(diagonal, own_s4, 0.0)
    row = lax.broadcasted_iota(jnp.int32, (size, modes), 0)
    starts = list(range(0, tile, size))
    befores = [lane < offset + start for start in starts]
    stack = jnp.concatenate(
        [
            part
            for before in befores
            for part in (
                jnp.where(before, over2, 0.0),
                jnp.where(before, over4, 0.0),
                jnp.where(before, 0.0, project_t),
            )
        ],
        axis=0,
    )
    sums = exact_nt(stack, project_t)
    blocks = []
    for n in range(len(starts)):
        at2, at4, after = (
            sums[(3 * n + m) * snap_count : (3 * n + m + 1) * snap_count] for m in range(3)
        )
        blocks.append(
            jnp.concatenate(
                [
                    jnp.concatenate([-(after + gram), at2 + eye], axis=1),
                    jnp.concatenate([at2 + eye, at4], axis=1),
                ],
                axis=0,
            )
        )
    lefts, rests = [], []
    for start, before, (change, entries) in zip(starts, befores, paired_inverses(blocks, 4)):
        image = exact_nn(change, joined)
        top, bottom = image[:snap_count], image[snap_count:]
        a, b, c = (jnp.broadcast_to(value[:, :1], top.shape) for value in entries)
        solved = jnp.concatenate([a * top + b * bottom, b * top + c * bottom], axis=0)
        stop = start + size
        mine = jnp.where(first_core, image[:, :tile], image[:, tile:])[:, start:stop]
        solved_mine = jnp.where(first_core, solved[:, :tile], solved[:, tile:])[:, start:stop]
        lefts.append(own_diagonal[start:stop, start:stop] + exact_tn(mine, solved_mine))
        rests.append(
            (lane == offset + start + row).astype(f32)
            - exact_tn(mine, jnp.where(before, solved / s4, 0.0))
        )
    smalls = inverse_factors(lefts, 8)
    return jnp.concatenate([exact_nn(small, rest) for small, rest in zip(smalls, rests)], axis=0)


def rotate_kernel(
    cells,
    hi, lo, total, singular, volumes,
    new_out, singular_out, hankel_out,
    rows_hi, rows_lo, result, root, in_sem, out_sem,
):
    tile, width = result.shape
    modes = 2 * tile
    snap_count = hi.shape[0] - modes
    near = tile + snap_count
    chunks = width // CHUNK
    core = lax.axis_index("mode")
    first_core = core == 0

    def piece(k):
        return pl.ds(pl.multiple_of(k * CHUNK, CHUNK), CHUNK)

    def loads(k):
        cols = piece(k)
        return (
            pltpu.make_async_copy(hi.at[:, cols], rows_hi.at[:, cols], in_sem.at[0, k]),
            pltpu.make_async_copy(lo.at[:, cols], rows_lo.at[:, cols], in_sem.at[1, k]),
        )

    for k in range(chunks):
        for copy in loads(k):
            copy.start()
    root[...] = lax.rsqrt(volumes[...] * (1.0 / cells))

    s = singular[...]
    s2 = s * s
    mid = tile // 2

    def get(which, row, count):
        flat = total.shape[2]
        first = row // flat
        return total[which, first : first + count // flat].reshape(count, tile)

    def both_cores(row, count):
        mine, others = get(0, row, count), get(1, row, count)
        return jnp.where(first_core, mine, others), jnp.where(first_core, others, mine)

    halves = both_cores(tile + mid, snap_count)
    project_t = jnp.concatenate(halves, axis=1)
    low_diagonal, low_corner = both_cores(0, mid), both_cores(mid, mid)
    snap_square = sum(value[:snap_count, mid : mid + snap_count] for value in low_corner)
    lower = jnp.concatenate(both_cores(tile, mid), axis=0)
    between = exact_nn(halves[1], lower)
    diagonal = jnp.zeros((snap_count, snap_count), f32)
    one_side = exact_nt(between, halves[0])
    for part, ends, corner in zip(halves, low_diagonal, low_corner):
        ahead, behind = part[:, :mid], part[:, mid:]
        diagonal += exact_nt(exact_nn(ahead, ends[:, :mid]), ahead)
        diagonal += exact_nt(exact_nn(behind, ends[:, mid:]), behind)
        one_side += exact_nt(exact_nn(behind, corner[:, :mid]), ahead)
    scaled_t = project_t * s2
    pad = jnp.zeros((tile - 2 * snap_count, modes), f32)
    turned = jnp.concatenate([project_t, scaled_t, pad], axis=0).T
    by_mode, by_mode_scaled = turned[:, :snap_count], turned[:, snap_count : 2 * snap_count]
    square = exact_nt(project_t, project_t)
    gram = (snap_square - 2.0 * square) + (diagonal + (one_side + one_side.T))
    pad = jnp.zeros((tile - 2 * snap_count, modes), f32)
    turned = jnp.concatenate([project_t, project_t * s2, pad], axis=0).T
    by_mode, by_mode_scaled = turned[:, :snap_count], turned[:, snap_count : 2 * snap_count]
    side = by_mode_scaled + exact_nn(by_mode, square + gram)
    side_and_project = jnp.concatenate([side, by_mode], axis=1)
    mine = own_inverse(project_t, s2, gram, first_core)
    both = exact_nn(mine, side_and_project)
    on_snaps = both[:, snap_count:]
    on_modes = mine * s2
    image = (on_modes + exact_nn(on_snaps, project_t)) * s
    energy = exact_nt(jnp.ones((8, modes), f32), image * image) + exact_nt(
        jnp.ones((8, snap_count), f32), both[:, :snap_count] * both[:, :snap_count]
    )
    singular_out[...] = jnp.sqrt(energy[:1])

    on_first, on_second = on_modes[:, :tile], on_modes[:, tile:]
    coef = split(
        jnp.concatenate(
            [
                jnp.where(first_core, on_first, on_second),
                on_snaps,
                jnp.where(first_core, on_second, on_first),
            ],
            axis=1,
        )
    )

    def rotate(k, carry):
        for copy in loads(k):
            copy.wait()
        cols = piece(k)
        value = dot3_nn(coef, (rows_hi[:, cols], rows_lo[:, cols]))
        result[:, cols] = value * root[:, cols]
        pltpu.make_async_copy(result.at[:, cols], new_out.at[:, cols], out_sem.at[k]).start()
        return carry

    lax.fori_loop(0, chunks, rotate, 0)

    base = tile + mid + snap_count
    swapped = (get(1, base + tile, tile), get(1, base + modes, snap_count), get(1, base, tile))
    straight = (get(0, base, tile), get(0, base + modes, snap_count), get(0, base + tile, tile))
    columns = jnp.concatenate(
        [
            jnp.concatenate(
                [jnp.where(first_core, a, b), jnp.where(first_core, b, a)], axis=1
            )
            for a, b in zip(straight, swapped)
        ],
        axis=0,
    )
    hankel_out[...] = dot3_nn(coef, split(columns))

    def finish(k, carry):
        pltpu.make_async_copy(result.at[:, piece(k)], new_out.at[:, piece(k)], out_sem.at[k]).wait()
        return carry

    lax.fori_loop(0, chunks, finish, 0)


def rotate(cells, hi, lo, total, singular, volumes):
    rows, width = hi.shape
    modes = singular.shape[1]
    tile = modes // 2
    chunks = width // CHUNK
    dma = pltpu.SemaphoreType.DMA
    vmem = pltpu.VMEM
    any_spec = pl.BlockSpec(memory_space=pl.ANY)
    vmem_spec = pl.BlockSpec(memory_space=vmem)
    return pl.pallas_call(
        functools.partial(rotate_kernel, cells),
        out_shape=(
            jax.ShapeDtypeStruct((tile, width), f32),
            jax.ShapeDtypeStruct((1, tile), f32),
            jax.ShapeDtypeStruct((tile, modes), f32),
        ),
        in_specs=[any_spec] * 2 + [vmem_spec] * 3,
        out_specs=(any_spec, vmem_spec, vmem_spec),
        scratch_shapes=[
            vmem((rows, width), bf16),
            vmem((rows, width), bf16),
            vmem((tile, width), f32),
            vmem((1, width), f32),
            dma((2, chunks)),
            dma((chunks,)),
        ],
        compiler_params=pltpu.CompilerParams(vmem_limit_bytes=56 * 1024 * 1024),
    )(hi, lo, total, singular, volumes)


def shards(basis, adjoint, snapshots, volumes, singular):
    tile, width = basis.shape
    cells = float(width * lax.axis_size("space"))
    volumes = volumes.reshape(1, width)
    hi, lo, total = gather(cells, basis, adjoint, snapshots, volumes)
    new_tile, new_singular, hankel = rotate(
        cells, hi, lo, total, singular.reshape(1, 2 * tile), volumes
    )
    return new_tile, new_singular.reshape(tile), hankel


def solution(mesh):
    return jax.shard_map(
        shards,
        mesh=mesh,
        in_specs=(P("mode", "space"), P("mode", "space"), P("mode", "space"), P("space"), P()),
        out_specs=(P("mode", "space"), P("mode"), P("mode", None)),
        check_vma=False,
    )
```

```python
import functools

import jax
import jax.numpy as jnp
from jax import lax
from jax.experimental import pallas as pl
from jax.experimental.pallas import tpu as pltpu
from jax.sharding import PartitionSpec as P

MESH = pl.DeviceIdType.MESH
highest = lax.Precision.HIGHEST
f32 = jnp.float32
bf16 = jnp.bfloat16
SIDE = 4
PLANE = SIDE * SIDE
CHUNK = 1024
TURN = 2048


def split(value):
    high = value.astype(bf16)
    return high, (value - high.astype(f32)).astype(bf16)


def dot_nt(left, right):
    return lax.dot_general(left, right, (((1,), (1,)), ((), ())), preferred_element_type=f32)


def dot3(left, right):
    return dot_nt(left[0], right[0]) + (dot_nt(left[0], right[1]) + dot_nt(left[1], right[0]))


def exact_nt(left, right):
    return lax.dot_general(
        left, right, (((1,), (1,)), ((), ())), precision=highest, preferred_element_type=f32
    )


def exact_nn(left, right):
    return lax.dot_general(
        left, right, (((1,), (0,)), ((), ())), precision=highest, preferred_element_type=f32
    )


def gather_kernel(
    cells,
    basis, adjoint, snaps, volumes,
    hi_out, lo_out, total,
    own, other, adj, snap, root,
    left_hi, left_lo, right_hi, right_lo,
    acc, acc_snap, share, slots, part, z_slots,
    load_sem, adj_sem, small_sem, bs_sem, br_sem, ss_sem, out_sem,
    rs_sem, rr_sem, zs_sem, zr_sem, gs_sem, gr_sem, fs_sem, fr_sem,
):
    tile, width = own.shape
    snap_count = snap.shape[0]
    half = snap_count // 2
    chunks = width // CHUNK
    near = tile + snap_count
    place = lax.axis_index("space")
    core = lax.axis_index("mode")
    pair = (place, 1 - core)
    spot = lax.rem(place, PLANE)
    level = place // PLANE

    def in_plane(step):
        return lax.rem(spot + step, PLANE)

    def plane_peer(step):
        return (level * PLANE + in_plane(step), core)

    def level_peer(step):
        return (lax.rem(level + step, SIDE) * PLANE + spot, core)

    def piece(k):
        return pl.ds(pl.multiple_of(k * CHUNK, CHUNK), CHUNK)

    def load_own(k):
        return pltpu.make_async_copy(basis.at[:, piece(k)], own.at[:, piece(k)], load_sem.at[k])

    def load_adj(k):
        return pltpu.make_async_copy(adjoint.at[:, piece(k)], adj.at[:, piece(k)], adj_sem.at[k])

    def remote(src, dst, send_sem, recv_sem, device):
        return pltpu.make_async_remote_copy(
            src_ref=src, dst_ref=dst, send_sem=send_sem, recv_sem=recv_sem,
            device_id=device, device_id_type=MESH,
        )

    barrier = pltpu.get_barrier_semaphore()
    friends = [pair]
    friends += [plane_peer(step) for step in range(1, PLANE)]
    friends += [level_peer(step) for step in range(1, SIDE)]
    for friend in friends:
        pl.semaphore_signal(barrier, inc=1, device_id=friend, device_id_type=MESH)
    snap_rows = pl.ds(pl.multiple_of(core * half, half), half)
    load_snap = pltpu.make_async_copy(snaps, snap.at[snap_rows], small_sem.at[0])
    load_snap.start()
    for k in range(chunks):
        load_own(k).start()
        load_adj(k).start()
    root[...] = jnp.sqrt(volumes[...] * (1.0 / cells))
    acc[...] = jnp.zeros_like(acc)
    acc_snap[...] = jnp.zeros_like(acc_snap)

    pl.semaphore_wait(barrier, len(friends))
    send_snap = remote(snaps, snap.at[snap_rows], ss_sem.at[0], ss_sem.at[1], pair)
    send_snap.start()

    def send_own(k):
        return remote(basis.at[:, piece(k)], other.at[:, piece(k)], bs_sem.at[k], br_sem.at[k], pair)

    for k in range(chunks):
        send_own(k).start()

    def prepare(k, carry):
        cols = piece(k)
        load_own(k).wait()
        high, low = split(own[:, cols] * root[:, cols])
        left_hi[:tile, cols], left_lo[:tile, cols] = high, low
        right_hi[:tile, cols], right_lo[:tile, cols] = high, low
        load_adj(k).wait()
        right_hi[tile:, cols], right_lo[tile:, cols] = split(adj[:, cols] * root[:, cols])
        return carry

    lax.fori_loop(0, chunks, prepare, 0)
    load_snap.wait()
    send_snap.wait()
    left_hi[tile:near], left_lo[tile:near] = split(snap[...] * root[...])

    def saves(k):
        cols = piece(k)
        return (
            pltpu.make_async_copy(left_hi.at[:, cols], hi_out.at[:, cols], out_sem.at[0, k]),
            pltpu.make_async_copy(left_lo.at[:, cols], lo_out.at[:, cols], out_sem.at[1, k]),
        )

    def multiply(k, carry):
        cols = piece(k)
        send_own(k).wait_recv()
        left_hi[near:, cols], left_lo[near:, cols] = split(other[:, cols] * root[:, cols])
        for copy in saves(k):
            copy.start()
        right = (right_hi[:, cols], right_lo[:, cols])
        acc[...] += dot3((left_hi[:, cols], left_lo[:, cols]), right)
        both = (left_hi[tile:near, cols], left_lo[tile:near, cols])
        acc_snap[...] += dot3(both, both)
        return carry

    lax.fori_loop(0, chunks, multiply, 0)

    mid = tile // 2
    flat = share.shape[1]

    def put(row, value):
        for start in range(0, value.shape[0], flat):
            share[(row + start) // flat] = value[start : start + flat]

    put(0, jnp.concatenate([acc[:mid, :mid], acc[mid:tile, mid:tile]], axis=1))
    snap_square = jnp.concatenate(
        [0.5 * acc_snap[...], jnp.zeros((mid - snap_count, snap_count), f32)], axis=0
    )
    put(
        mid,
        jnp.concatenate(
            [acc[mid:tile, :mid], snap_square, jnp.zeros((mid, mid - snap_count), f32)], axis=1
        ),
    )
    mixed = acc[near:, :tile]
    put(tile, jnp.where(core == 0, mixed[:mid], mixed.T[mid:]))
    put(tile + mid, acc[tile:near, :tile])
    put(tile + mid + snap_count, acc[:tile, tile:])
    put(2 * tile + mid + snap_count, acc[near:, tile:])
    put(3 * tile + mid + snap_count, acc[tile:near, tile:])

    copies = [
        remote(share.at[in_plane(step)], slots.at[step], rs_sem.at[step], rr_sem.at[step],
               plane_peer(step))
        for step in range(1, PLANE)
    ]
    for copy in copies:
        copy.start()
    slots[0] = share[spot]
    for copy in copies:
        copy.wait_recv()
    value = slots[: PLANE // 2] + slots[PLANE // 2 :]
    value = value[: PLANE // 4] + value[PLANE // 4 :]
    value = value[: PLANE // 8] + value[PLANE // 8 :]
    part[0] = value[0] + value[1]

    z_copies = [
        remote(part.at[0], z_slots.at[step], zs_sem.at[step], zr_sem.at[step], level_peer(step))
        for step in range(1, SIDE)
    ]
    for copy in z_copies:
        copy.start()
    for copy in z_copies:
        copy.wait_recv()
    part[1] = (part[0] + z_slots[2]) + (z_slots[1] + z_slots[3])

    g_copies = [
        remote(part.at[1], total.at[0, spot], gs_sem.at[step], gr_sem.at[step], plane_peer(step))
        for step in range(1, PLANE)
    ]
    for copy in g_copies:
        copy.start()
    f_copies = [remote(part.at[1], total.at[1, spot], fs_sem.at[0], fr_sem.at[0], pair)]
    f_copies[0].start()
    total[0, spot] = part[1]
    for step in range(1, PLANE):
        source = in_plane(PLANE - step)
        remote(part.at[1], total.at[0, source], gs_sem.at[step], gr_sem.at[step], pair).wait_recv()
        f_copies.append(
            remote(total.at[0, source], total.at[1, source], fs_sem.at[step], fr_sem.at[step], pair)
        )
        f_copies[-1].start()
    for copy in f_copies:
        copy.wait()
    for copy in copies + z_copies + g_copies:
        copy.wait_send()

    def finish(k, carry):
        send_own(k).wait_send()
        for copy in saves(k):
            copy.wait()
        return carry

    lax.fori_loop(0, chunks, finish, 0)


def gather(cells, basis, adjoint, snapshots, volumes):
    tile, width = basis.shape
    snap_count = 2 * snapshots.shape[0]
    rows = 2 * tile + snap_count
    flat = (7 * tile // 2 + 2 * snap_count) // PLANE
    chunks = width // CHUNK
    dma = pltpu.SemaphoreType.DMA
    vmem = pltpu.VMEM
    any_spec = pl.BlockSpec(memory_space=pl.ANY)
    vmem_spec = pl.BlockSpec(memory_space=vmem)
    return pl.pallas_call(
        functools.partial(gather_kernel, cells),
        out_shape=(
            jax.ShapeDtypeStruct((rows, width), bf16),
            jax.ShapeDtypeStruct((rows, width), bf16),
            jax.ShapeDtypeStruct((2, PLANE, flat, tile), f32),
        ),
        in_specs=[any_spec, any_spec, any_spec, vmem_spec],
        out_specs=(any_spec, any_spec, vmem_spec),
        scratch_shapes=[
            vmem((tile, width), f32),
            vmem((tile, width), f32),
            vmem((tile, width), f32),
            vmem((snap_count, width), f32),
            vmem((1, width), f32),
            vmem((rows, width), bf16),
            vmem((rows, width), bf16),
            vmem((2 * tile, width), bf16),
            vmem((2 * tile, width), bf16),
            vmem((rows, 2 * tile), f32),
            vmem((snap_count, snap_count), f32),
            vmem((PLANE, flat, tile), f32),
            vmem((PLANE, flat, tile), f32),
            vmem((2, flat, tile), f32),
            vmem((SIDE, flat, tile), f32),
            dma((chunks,)),
            dma((chunks,)),
            dma((1,)),
            dma((chunks,)),
            dma((chunks,)),
            dma((2,)),
            dma((2, chunks)),
            dma((PLANE,)),
            dma((PLANE,)),
            dma((SIDE,)),
            dma((SIDE,)),
            dma((PLANE,)),
            dma((PLANE,)),
            dma((PLANE,)),
            dma((PLANE,)),
        ],
        compiler_params=pltpu.CompilerParams(
            collective_id=0, has_side_effects=True, vmem_limit_bytes=56 * 1024 * 1024
        ),
    )(basis, adjoint, snapshots, volumes)


def dot_nn(left, right):
    return lax.dot_general(left, right, (((1,), (0,)), ((), ())), preferred_element_type=f32)


def dot3_nn(left, right):
    rows = left[0].shape[0]
    both = dot_nn(jnp.concatenate([left[0], left[1]], axis=0), right[0])
    return both[:rows] + (dot_nn(left[0], right[1]) + both[rows:])


def exact_tn(left, right):
    return lax.dot_general(
        left, right, (((0,), (0,)), ((), ())), precision=highest, preferred_element_type=f32
    )


def inverse_factors(blocks, group):
    size = blocks[0].shape[0]
    width = 2 * size
    eye = (
        lax.broadcasted_iota(jnp.int32, (size, size), 0)
        == lax.broadcasted_iota(jnp.int32, (size, size), 1)
    ).astype(f32)
    lefts = [jnp.concatenate([block, eye], axis=1) for block in blocks]
    done = [[] for _ in blocks]
    for start in range(0, size, group):
        count = size - start
        row = lax.broadcasted_iota(jnp.int32, (count, width), 0)
        cols = [
            [
                jnp.broadcast_to(left[:, start + t : start + t + 1], (count, width))
                for t in range(group)
            ]
            for left in lefts
        ]
        for t in range(group):
            for n, col in enumerate(cols):
                pivot = col[t][t : t + 1, :]
                factor = jnp.where(row > t, col[t], 0.0) * (1.0 / pivot)
                for u in range(t + 1, group):
                    col[u] = col[u] - factor * col[u][t : t + 1, :]
                done[n].append(lefts[n][t : t + 1, :] * lax.rsqrt(pivot))
                lefts[n] = lefts[n] - factor * lefts[n][t : t + 1, :]
        lefts = [left[group:] for left in lefts]
    return [jnp.concatenate(rows, axis=0)[:, size:] for rows in done]


def paired_inverses(blocks, group):
    size = blocks[0].shape[0]
    half, width = size // 2, 2 * size
    eye = (
        lax.broadcasted_iota(jnp.int32, (size, size), 0)
        == lax.broadcasted_iota(jnp.int32, (size, size), 1)
    ).astype(f32)
    lefts = [jnp.concatenate([block, eye], axis=1) for block in blocks]
    row = lax.broadcasted_iota(jnp.int32, (size, width), 0)
    row = jnp.where(row >= half, row - half, row)
    entries = [([], [], []) for _ in blocks]
    for start in range(0, half, group):
        places = list(range(start, start + group)) + list(range(half + start, half + start + group))
        cols = [
            [jnp.broadcast_to(left[:, at : at + 1], (size, width)) for at in places] for left in lefts
        ]
        for t in range(group):
            at = start + t
            upper, lower = slice(at, at + 1), slice(half + at, half + at + 1)
            below = row > at
            for n, col in enumerate(cols):
                first, second = col[t], col[group + t]
                alpha, beta, delta = first[upper], second[upper], second[lower]
                scale = 1.0 / (alpha * delta - beta * beta)
                a, b, c = delta * scale, -(beta * scale), alpha * scale
                for kept, value in zip(entries[n], (a, b, c)):
                    kept.append(value)
                on_upper = jnp.where(below, first * a + second * b, 0.0)
                on_lower = jnp.where(below, first * b + second * c, 0.0)
                for u in list(range(t + 1, group)) + list(range(group + t + 1, 2 * group)):
                    col[u] = col[u] - (on_upper * col[u][upper] + on_lower * col[u][lower])
                lefts[n] = lefts[n] - (on_upper * lefts[n][upper] + on_lower * lefts[n][lower])
    return [
        (left[:, size:], [jnp.concatenate(kept, axis=0) for kept in kinds])
        for left, kinds in zip(lefts, entries)
    ]


def own_inverse(project_t, s2, gram, first_core):
    snap_count, modes = project_t.shape
    tile, size = modes // 2, 64
    lane = lax.broadcasted_iota(jnp.int32, (1, modes), 1)
    offset = jnp.where(first_core, 0, tile)
    s4 = s2 * s2
    joined = jnp.concatenate([project_t * s2, project_t], axis=0)
    over2, over4 = project_t / s2, project_t / s4
    eye = (
        lax.broadcasted_iota(jnp.int32, (snap_count, snap_count), 0)
        == lax.broadcasted_iota(jnp.int32, (snap_count, snap_count), 1)
    ).astype(f32)
    diagonal = (
        lax.broadcasted_iota(jnp.int32, (tile, tile), 0)
        == lax.broadcasted_iota(jnp.int32, (tile, tile), 1)
    )
    own_s4 = jnp.where(first_core, s4[:, :tile], s4[:, tile:])
    own_diagonal = jnp.where(diagonal, own_s4, 0.0)
    row = lax.broadcasted_iota(jnp.int32, (size, modes), 0)
    starts = list(range(0, tile, size))
    befores = [lane < offset + start for start in starts]
    stack = jnp.concatenate(
        [
            part
            for before in befores
            for part in (
                jnp.where(before, over2, 0.0),
                jnp.where(before, over4, 0.0),
                jnp.where(before, 0.0, project_t),
            )
        ],
        axis=0,
    )
    sums = exact_nt(stack, project_t)
    blocks = []
    for n in range(len(starts)):
        at2, at4, after = (
            sums[(3 * n + m) * snap_count : (3 * n + m + 1) * snap_count] for m in range(3)
        )
        blocks.append(
            jnp.concatenate(
                [
                    jnp.concatenate([-(after + gram), at2 + eye], axis=1),
                    jnp.concatenate([at2 + eye, at4], axis=1),
                ],
                axis=0,
            )
        )
    lefts, rests = [], []
    for start, before, (change, entries) in zip(starts, befores, paired_inverses(blocks, 4)):
        image = exact_nn(change, joined)
        top, bottom = image[:snap_count], image[snap_count:]
        a, b, c = (jnp.broadcast_to(value[:, :1], top.shape) for value in entries)
        solved = jnp.concatenate([a * top + b * bottom, b * top + c * bottom], axis=0)
        stop = start + size
        mine = jnp.where(first_core, image[:, :tile], image[:, tile:])[:, start:stop]
        solved_mine = jnp.where(first_core, solved[:, :tile], solved[:, tile:])[:, start:stop]
        lefts.append(own_diagonal[start:stop, start:stop] + exact_tn(mine, solved_mine))
        rests.append(
            (lane == offset + start + row).astype(f32)
            - exact_tn(mine, jnp.where(before, solved / s4, 0.0))
        )
    smalls = inverse_factors(lefts, 8)
    return jnp.concatenate([exact_nn(small, rest) for small, rest in zip(smalls, rests)], axis=0)


def rotate_kernel(
    cells,
    hi, lo, total, singular, volumes,
    new_out, singular_out, hankel_out,
    rows_hi, rows_lo, result, root, in_sem, out_sem,
):
    tile, width = result.shape
    modes = 2 * tile
    snap_count = hi.shape[0] - modes
    near = tile + snap_count
    chunks = width // TURN
    core = lax.axis_index("mode")
    first_core = core == 0

    def piece(k):
        return pl.ds(pl.multiple_of(k * TURN, TURN), TURN)

    def loads(k):
        cols = piece(k)
        return (
            pltpu.make_async_copy(hi.at[:, cols], rows_hi.at[:, cols], in_sem.at[0, k]),
            pltpu.make_async_copy(lo.at[:, cols], rows_lo.at[:, cols], in_sem.at[1, k]),
        )

    for k in range(chunks):
        for copy in loads(k):
            copy.start()
    root[...] = lax.rsqrt(volumes[...] * (1.0 / cells))

    s = singular[...]
    s2 = s * s
    mid = tile // 2

    def get(which, row, count):
        flat = total.shape[2]
        first = row // flat
        return total[which, first : first + count // flat].reshape(count, tile)

    def both_cores(row, count):
        mine, others = get(0, row, count), get(1, row, count)
        return jnp.where(first_core, mine, others), jnp.where(first_core, others, mine)

    halves = both_cores(tile + mid, snap_count)
    project_t = jnp.concatenate(halves, axis=1)
    low_diagonal, low_corner = both_cores(0, mid), both_cores(mid, mid)
    snap_square = sum(value[:snap_count, mid : mid + snap_count] for value in low_corner)
    lower = jnp.concatenate(both_cores(tile, mid), axis=0)
    between = exact_nn(halves[1], lower)
    diagonal = jnp.zeros((snap_count, snap_count), f32)
    one_side = exact_nt(between, halves[0])
    for part, ends, corner in zip(halves, low_diagonal, low_corner):
        ahead, behind = part[:, :mid], part[:, mid:]
        diagonal += exact_nt(exact_nn(ahead, ends[:, :mid]), ahead)
        diagonal += exact_nt(exact_nn(behind, ends[:, mid:]), behind)
        one_side += exact_nt(exact_nn(behind, corner[:, :mid]), ahead)
    scaled_t = project_t * s2
    pad = jnp.zeros((tile - 2 * snap_count, modes), f32)
    turned = jnp.concatenate([project_t, scaled_t, pad], axis=0).T
    by_mode, by_mode_scaled = turned[:, :snap_count], turned[:, snap_count : 2 * snap_count]
    square = exact_nt(project_t, project_t)
    gram = (snap_square - 2.0 * square) + (diagonal + (one_side + one_side.T))
    pad = jnp.zeros((tile - 2 * snap_count, modes), f32)
    turned = jnp.concatenate([project_t, project_t * s2, pad], axis=0).T
    by_mode, by_mode_scaled = turned[:, :snap_count], turned[:, snap_count : 2 * snap_count]
    side = by_mode_scaled + exact_nn(by_mode, square + gram)
    side_and_project = jnp.concatenate([side, by_mode], axis=1)
    mine = own_inverse(project_t, s2, gram, first_core)
    both = exact_nn(mine, side_and_project)
    on_snaps = both[:, snap_count:]
    on_modes = mine * s2
    image = (on_modes + exact_nn(on_snaps, project_t)) * s
    energy = exact_nt(jnp.ones((8, modes), f32), image * image) + exact_nt(
        jnp.ones((8, snap_count), f32), both[:, :snap_count] * both[:, :snap_count]
    )
    singular_out[...] = jnp.sqrt(energy[:1])

    on_first, on_second = on_modes[:, :tile], on_modes[:, tile:]
    coef = split(
        jnp.concatenate(
            [
                jnp.where(first_core, on_first, on_second),
                on_snaps,
                jnp.where(first_core, on_second, on_first),
            ],
            axis=1,
        )
    )

    def rotate(k, carry):
        for copy in loads(k):
            copy.wait()
        cols = piece(k)
        value = dot3_nn(coef, (rows_hi[:, cols], rows_lo[:, cols]))
        result[:, cols] = value * root[:, cols]
        pltpu.make_async_copy(result.at[:, cols], new_out.at[:, cols], out_sem.at[k]).start()
        return carry

    lax.fori_loop(0, chunks, rotate, 0)

    base = tile + mid + snap_count
    swapped = (get(1, base + tile, tile), get(1, base + modes, snap_count), get(1, base, tile))
    straight = (get(0, base, tile), get(0, base + modes, snap_count), get(0, base + tile, tile))
    columns = jnp.concatenate(
        [
            jnp.concatenate(
                [jnp.where(first_core, a, b), jnp.where(first_core, b, a)], axis=1
            )
            for a, b in zip(straight, swapped)
        ],
        axis=0,
    )
    hankel_out[...] = dot3_nn(coef, split(columns))

    def finish(k, carry):
        pltpu.make_async_copy(result.at[:, piece(k)], new_out.at[:, piece(k)], out_sem.at[k]).wait()
        return carry

    lax.fori_loop(0, chunks, finish, 0)


def rotate(cells, hi, lo, total, singular, volumes):
    rows, width = hi.shape
    modes = singular.shape[1]
    tile = modes // 2
    chunks = width // TURN
    dma = pltpu.SemaphoreType.DMA
    vmem = pltpu.VMEM
    any_spec = pl.BlockSpec(memory_space=pl.ANY)
    vmem_spec = pl.BlockSpec(memory_space=vmem)
    return pl.pallas_call(
        functools.partial(rotate_kernel, cells),
        out_shape=(
            jax.ShapeDtypeStruct((tile, width), f32),
            jax.ShapeDtypeStruct((1, tile), f32),
            jax.ShapeDtypeStruct((tile, modes), f32),
        ),
        in_specs=[any_spec] * 2 + [vmem_spec] * 3,
        out_specs=(any_spec, vmem_spec, vmem_spec),
        scratch_shapes=[
            vmem((rows, width), bf16),
            vmem((rows, width), bf16),
            vmem((tile, width), f32),
            vmem((1, width), f32),
            dma((2, chunks)),
            dma((chunks,)),
        ],
        compiler_params=pltpu.CompilerParams(vmem_limit_bytes=56 * 1024 * 1024),
    )(hi, lo, total, singular, volumes)


def shards(basis, adjoint, snapshots, volumes, singular):
    tile, width = basis.shape
    cells = float(width * lax.axis_size("space"))
    volumes = volumes.reshape(1, width)
    hi, lo, total = gather(cells, basis, adjoint, snapshots, volumes)
    new_tile, new_singular, hankel = rotate(
        cells, hi, lo, total, singular.reshape(1, 2 * tile), volumes
    )
    return new_tile, new_singular.reshape(tile), hankel


def solution(mesh):
    return jax.shard_map(
        shards,
        mesh=mesh,
        in_specs=(P("mode", "space"), P("mode", "space"), P("mode", "space"), P("space"), P()),
        out_specs=(P("mode", "space"), P("mode"), P("mode", None)),
        check_vma=False,
    )
```

```python
import functools

import jax
import jax.numpy as jnp
from jax import lax
from jax.experimental import pallas as pl
from jax.experimental.pallas import tpu as pltpu
from jax.sharding import PartitionSpec as P

MESH = pl.DeviceIdType.MESH
highest = lax.Precision.HIGHEST
f32 = jnp.float32
bf16 = jnp.bfloat16
SIDE = 4
PLANE = SIDE * SIDE
CHUNK = 1024
TURN = 2048


def split(value):
    high = value.astype(bf16)
    return high, (value - high.astype(f32)).astype(bf16)


def dot_nt(left, right):
    return lax.dot_general(left, right, (((1,), (1,)), ((), ())), preferred_element_type=f32)


def dot3(left, right):
    return dot_nt(left[0], right[0]) + (dot_nt(left[0], right[1]) + dot_nt(left[1], right[0]))


def exact_nt(left, right):
    return lax.dot_general(
        left, right, (((1,), (1,)), ((), ())), precision=highest, preferred_element_type=f32
    )


def exact_nn(left, right):
    return lax.dot_general(
        left, right, (((1,), (0,)), ((), ())), precision=highest, preferred_element_type=f32
    )


def gather_kernel(
    cells,
    basis, adjoint, snaps, volumes,
    hi_out, lo_out, total,
    own, other, adj, snap, root,
    left_hi, left_lo, right_hi, right_lo,
    acc, acc_snap, share, slots, part, z_slots,
    load_sem, adj_sem, small_sem, bs_sem, br_sem, ss_sem, out_sem,
    rs_sem, rr_sem, zs_sem, zr_sem, gs_sem, gr_sem, fs_sem, fr_sem,
):
    tile, width = own.shape
    snap_count = snap.shape[0]
    half = snap_count // 2
    chunks = width // CHUNK
    near = tile + snap_count
    place = lax.axis_index("space")
    core = lax.axis_index("mode")
    pair = (place, 1 - core)
    spot = lax.rem(place, PLANE)
    level = place // PLANE

    def in_plane(step):
        return lax.rem(spot + step, PLANE)

    def plane_peer(step):
        return (level * PLANE + in_plane(step), core)

    def level_peer(step):
        return (lax.rem(level + step, SIDE) * PLANE + spot, core)

    def piece(k):
        start = k * CHUNK
        return pl.ds(start if isinstance(k, int) else pl.multiple_of(start, CHUNK), CHUNK)

    def load_own(k):
        return pltpu.make_async_copy(basis.at[:, piece(k)], own.at[:, piece(k)], load_sem.at[k])

    def load_adj(k):
        return pltpu.make_async_copy(adjoint.at[:, piece(k)], adj.at[:, piece(k)], adj_sem.at[k])

    def remote(src, dst, send_sem, recv_sem, device):
        return pltpu.make_async_remote_copy(
            src_ref=src, dst_ref=dst, send_sem=send_sem, recv_sem=recv_sem,
            device_id=device, device_id_type=MESH,
        )

    barrier = pltpu.get_barrier_semaphore()
    friends = [pair]
    friends += [plane_peer(step) for step in range(1, PLANE)]
    friends += [level_peer(step) for step in range(1, SIDE)]
    for friend in friends:
        pl.semaphore_signal(barrier, inc=1, device_id=friend, device_id_type=MESH)
    snap_rows = pl.ds(pl.multiple_of(core * half, half), half)
    load_snap = pltpu.make_async_copy(snaps, snap.at[snap_rows], small_sem.at[0])
    load_snap.start()
    for k in range(chunks):
        load_own(k).start()
        load_adj(k).start()
    root[...] = jnp.sqrt(volumes[...] * (1.0 / cells))
    acc[...] = jnp.zeros_like(acc)
    acc_snap[...] = jnp.zeros_like(acc_snap)

    pl.semaphore_wait(barrier, len(friends))
    send_snap = remote(snaps, snap.at[snap_rows], ss_sem.at[0], ss_sem.at[1], pair)
    send_snap.start()

    def send_own(k):
        return remote(basis.at[:, piece(k)], other.at[:, piece(k)], bs_sem.at[k], br_sem.at[k], pair)

    for k in range(chunks):
        send_own(k).start()

    def prepare(k, carry):
        cols = piece(k)
        load_own(k).wait()
        high, low = split(own[:, cols] * root[:, cols])
        left_hi[:tile, cols], left_lo[:tile, cols] = high, low
        right_hi[:tile, cols], right_lo[:tile, cols] = high, low
        load_adj(k).wait()
        right_hi[tile:, cols], right_lo[tile:, cols] = split(adj[:, cols] * root[:, cols])
        return carry

    lax.fori_loop(0, chunks, prepare, 0)
    load_snap.wait()
    send_snap.wait()
    left_hi[tile:near], left_lo[tile:near] = split(snap[...] * root[...])

    def saves(k):
        cols = piece(k)
        return (
            pltpu.make_async_copy(left_hi.at[:, cols], hi_out.at[:, cols], out_sem.at[0, k]),
            pltpu.make_async_copy(left_lo.at[:, cols], lo_out.at[:, cols], out_sem.at[1, k]),
        )

    def multiply(k, carry):
        cols = piece(k)
        send_own(k).wait_recv()
        left_hi[near:, cols], left_lo[near:, cols] = split(other[:, cols] * root[:, cols])
        for copy in saves(k):
            copy.start()
        right = (right_hi[:, cols], right_lo[:, cols])
        acc[...] += dot3((left_hi[:, cols], left_lo[:, cols]), right)
        both = (left_hi[tile:near, cols], left_lo[tile:near, cols])
        acc_snap[...] += dot3(both, both)
        return carry

    lax.fori_loop(0, chunks - 1, multiply, 0)

    cols = piece(chunks - 1)
    right = (right_hi[:, cols], right_lo[:, cols])
    acc[:near] += dot3((left_hi[:near, cols], left_lo[:near, cols]), right)
    both = (left_hi[tile:near, cols], left_lo[tile:near, cols])
    acc_snap[...] += dot3(both, both)
    send_own(chunks - 1).wait_recv()
    left_hi[near:, cols], left_lo[near:, cols] = split(other[:, cols] * root[:, cols])
    for copy in saves(chunks - 1):
        copy.start()
    acc[near:] += dot3((left_hi[near:, cols], left_lo[near:, cols]), right)

    mid = tile // 2
    flat = share.shape[1]

    def put(row, value):
        for start in range(0, value.shape[0], flat):
            share[(row + start) // flat] = value[start : start + flat]

    put(0, jnp.concatenate([acc[:mid, :mid], acc[mid:tile, mid:tile]], axis=1))
    snap_square = jnp.concatenate(
        [0.5 * acc_snap[...], jnp.zeros((mid - snap_count, snap_count), f32)], axis=0
    )
    put(
        mid,
        jnp.concatenate(
            [acc[mid:tile, :mid], snap_square, jnp.zeros((mid, mid - snap_count), f32)], axis=1
        ),
    )
    mixed = acc[near:, :tile]
    put(tile, jnp.where(core == 0, mixed[:mid], mixed.T[mid:]))
    put(tile + mid, acc[tile:near, :tile])
    put(tile + mid + snap_count, acc[:tile, tile:])
    put(2 * tile + mid + snap_count, acc[near:, tile:])
    put(3 * tile + mid + snap_count, acc[tile:near, tile:])

    copies = [
        remote(share.at[in_plane(step)], slots.at[step], rs_sem.at[step], rr_sem.at[step],
               plane_peer(step))
        for step in range(1, PLANE)
    ]
    for copy in copies:
        copy.start()
    slots[0] = share[spot]
    for copy in copies:
        copy.wait_recv()
    value = slots[: PLANE // 2] + slots[PLANE // 2 :]
    value = value[: PLANE // 4] + value[PLANE // 4 :]
    value = value[: PLANE // 8] + value[PLANE // 8 :]
    part[0] = value[0] + value[1]

    z_copies = [
        remote(part.at[0], z_slots.at[step], zs_sem.at[step], zr_sem.at[step], level_peer(step))
        for step in range(1, SIDE)
    ]
    for copy in z_copies:
        copy.start()
    for copy in z_copies:
        copy.wait_recv()
    part[1] = (part[0] + z_slots[2]) + (z_slots[1] + z_slots[3])

    g_copies = [
        remote(part.at[1], total.at[0, spot], gs_sem.at[step], gr_sem.at[step], plane_peer(step))
        for step in range(1, PLANE)
    ]
    for copy in g_copies:
        copy.start()
    f_copies = [remote(part.at[1], total.at[1, spot], fs_sem.at[0], fr_sem.at[0], pair)]
    f_copies[0].start()
    total[0, spot] = part[1]
    for step in range(1, PLANE):
        source = in_plane(PLANE - step)
        remote(part.at[1], total.at[0, source], gs_sem.at[step], gr_sem.at[step], pair).wait_recv()
        f_copies.append(
            remote(total.at[0, source], total.at[1, source], fs_sem.at[step], fr_sem.at[step], pair)
        )
        f_copies[-1].start()
    for copy in f_copies:
        copy.wait()
    for copy in copies + z_copies + g_copies:
        copy.wait_send()

    def finish(k, carry):
        send_own(k).wait_send()
        for copy in saves(k):
            copy.wait()
        return carry

    lax.fori_loop(0, chunks, finish, 0)


def gather(cells, basis, adjoint, snapshots, volumes):
    tile, width = basis.shape
    snap_count = 2 * snapshots.shape[0]
    rows = 2 * tile + snap_count
    flat = (7 * tile // 2 + 2 * snap_count) // PLANE
    chunks = width // CHUNK
    dma = pltpu.SemaphoreType.DMA
    vmem = pltpu.VMEM
    any_spec = pl.BlockSpec(memory_space=pl.ANY)
    vmem_spec = pl.BlockSpec(memory_space=vmem)
    return pl.pallas_call(
        functools.partial(gather_kernel, cells),
        out_shape=(
            jax.ShapeDtypeStruct((rows, width), bf16),
            jax.ShapeDtypeStruct((rows, width), bf16),
            jax.ShapeDtypeStruct((2, PLANE, flat, tile), f32),
        ),
        in_specs=[any_spec, any_spec, any_spec, vmem_spec],
        out_specs=(any_spec, any_spec, vmem_spec),
        scratch_shapes=[
            vmem((tile, width), f32),
            vmem((tile, width), f32),
            vmem((tile, width), f32),
            vmem((snap_count, width), f32),
            vmem((1, width), f32),
            vmem((rows, width), bf16),
            vmem((rows, width), bf16),
            vmem((2 * tile, width), bf16),
            vmem((2 * tile, width), bf16),
            vmem((rows, 2 * tile), f32),
            vmem((snap_count, snap_count), f32),
            vmem((PLANE, flat, tile), f32),
            vmem((PLANE, flat, tile), f32),
            vmem((2, flat, tile), f32),
            vmem((SIDE, flat, tile), f32),
            dma((chunks,)),
            dma((chunks,)),
            dma((1,)),
            dma((chunks,)),
            dma((chunks,)),
            dma((2,)),
            dma((2, chunks)),
            dma((PLANE,)),
            dma((PLANE,)),
            dma((SIDE,)),
            dma((SIDE,)),
            dma((PLANE,)),
            dma((PLANE,)),
            dma((PLANE,)),
            dma((PLANE,)),
        ],
        compiler_params=pltpu.CompilerParams(
            collective_id=0, has_side_effects=True, vmem_limit_bytes=56 * 1024 * 1024
        ),
    )(basis, adjoint, snapshots, volumes)


def dot_nn(left, right):
    return lax.dot_general(left, right, (((1,), (0,)), ((), ())), preferred_element_type=f32)


def dot3_nn(left, right):
    rows = left[0].shape[0]
    both = dot_nn(jnp.concatenate([left[0], left[1]], axis=0), right[0])
    return both[:rows] + (dot_nn(left[0], right[1]) + both[rows:])


def exact_tn(left, right):
    return lax.dot_general(
        left, right, (((0,), (0,)), ((), ())), precision=highest, preferred_element_type=f32
    )


def inverse_factors(blocks, group):
    size = blocks[0].shape[0]
    width = 2 * size
    eye = (
        lax.broadcasted_iota(jnp.int32, (size, size), 0)
        == lax.broadcasted_iota(jnp.int32, (size, size), 1)
    ).astype(f32)
    lefts = [jnp.concatenate([block, eye], axis=1) for block in blocks]
    done = [[] for _ in blocks]
    for start in range(0, size, group):
        count = size - start
        row = lax.broadcasted_iota(jnp.int32, (count, width), 0)
        cols = [
            [
                jnp.broadcast_to(left[:, start + t : start + t + 1], (count, width))
                for t in range(group)
            ]
            for left in lefts
        ]
        for t in range(group):
            for n, col in enumerate(cols):
                pivot = col[t][t : t + 1, :]
                factor = jnp.where(row > t, col[t], 0.0) * (1.0 / pivot)
                for u in range(t + 1, group):
                    col[u] = col[u] - factor * col[u][t : t + 1, :]
                done[n].append(lefts[n][t : t + 1, :] * lax.rsqrt(pivot))
                lefts[n] = lefts[n] - factor * lefts[n][t : t + 1, :]
        lefts = [left[group:] for left in lefts]
    return [jnp.concatenate(rows, axis=0)[:, size:] for rows in done]


def paired_inverses(blocks, group):
    size = blocks[0].shape[0]
    half, width = size // 2, 2 * size
    eye = (
        lax.broadcasted_iota(jnp.int32, (size, size), 0)
        == lax.broadcasted_iota(jnp.int32, (size, size), 1)
    ).astype(f32)
    lefts = [jnp.concatenate([block, eye], axis=1) for block in blocks]
    row = lax.broadcasted_iota(jnp.int32, (size, width), 0)
    row = jnp.where(row >= half, row - half, row)
    entries = [([], [], []) for _ in blocks]
    for start in range(0, half, group):
        places = list(range(start, start + group)) + list(range(half + start, half + start + group))
        cols = [
            [jnp.broadcast_to(left[:, at : at + 1], (size, width)) for at in places] for left in lefts
        ]
        for t in range(group):
            at = start + t
            upper, lower = slice(at, at + 1), slice(half + at, half + at + 1)
            below = row > at
            for n, col in enumerate(cols):
                first, second = col[t], col[group + t]
                alpha, beta, delta = first[upper], second[upper], second[lower]
                scale = 1.0 / (alpha * delta - beta * beta)
                a, b, c = delta * scale, -(beta * scale), alpha * scale
                for kept, value in zip(entries[n], (a, b, c)):
                    kept.append(value)
                on_upper = jnp.where(below, first * a + second * b, 0.0)
                on_lower = jnp.where(below, first * b + second * c, 0.0)
                for u in list(range(t + 1, group)) + list(range(group + t + 1, 2 * group)):
                    col[u] = col[u] - (on_upper * col[u][upper] + on_lower * col[u][lower])
                lefts[n] = lefts[n] - (on_upper * lefts[n][upper] + on_lower * lefts[n][lower])
    return [
        (left[:, size:], [jnp.concatenate(kept, axis=0) for kept in kinds])
        for left, kinds in zip(lefts, entries)
    ]


def own_inverse(project_t, s2, gram, first_core):
    snap_count, modes = project_t.shape
    tile, size = modes // 2, 64
    lane = lax.broadcasted_iota(jnp.int32, (1, modes), 1)
    offset = jnp.where(first_core, 0, tile)
    s4 = s2 * s2
    joined = jnp.concatenate([project_t * s2, project_t], axis=0)
    over2, over4 = project_t / s2, project_t / s4
    eye = (
        lax.broadcasted_iota(jnp.int32, (snap_count, snap_count), 0)
        == lax.broadcasted_iota(jnp.int32, (snap_count, snap_count), 1)
    ).astype(f32)
    diagonal = (
        lax.broadcasted_iota(jnp.int32, (tile, tile), 0)
        == lax.broadcasted_iota(jnp.int32, (tile, tile), 1)
    )
    own_s4 = jnp.where(first_core, s4[:, :tile], s4[:, tile:])
    own_diagonal = jnp.where(diagonal, own_s4, 0.0)
    row = lax.broadcasted_iota(jnp.int32, (size, modes), 0)
    starts = list(range(0, tile, size))
    befores = [lane < offset + start for start in starts]
    stack = jnp.concatenate(
        [
            part
            for before in befores
            for part in (
                jnp.where(before, over2, 0.0),
                jnp.where(before, over4, 0.0),
                jnp.where(before, 0.0, project_t),
            )
        ],
        axis=0,
    )
    sums = exact_nt(stack, project_t)
    blocks = []
    for n in range(len(starts)):
        at2, at4, after = (
            sums[(3 * n + m) * snap_count : (3 * n + m + 1) * snap_count] for m in range(3)
        )
        blocks.append(
            jnp.concatenate(
                [
                    jnp.concatenate([-(after + gram), at2 + eye], axis=1),
                    jnp.concatenate([at2 + eye, at4], axis=1),
                ],
                axis=0,
            )
        )
    lefts, rests = [], []
    for start, before, (change, entries) in zip(starts, befores, paired_inverses(blocks, 4)):
        image = exact_nn(change, joined)
        top, bottom = image[:snap_count], image[snap_count:]
        a, b, c = (jnp.broadcast_to(value[:, :1], top.shape) for value in entries)
        solved = jnp.concatenate([a * top + b * bottom, b * top + c * bottom], axis=0)
        stop = start + size
        mine = jnp.where(first_core, image[:, :tile], image[:, tile:])[:, start:stop]
        solved_mine = jnp.where(first_core, solved[:, :tile], solved[:, tile:])[:, start:stop]
        lefts.append(own_diagonal[start:stop, start:stop] + exact_tn(mine, solved_mine))
        rests.append(
            (lane == offset + start + row).astype(f32)
            - exact_tn(mine, jnp.where(before, solved / s4, 0.0))
        )
    smalls = inverse_factors(lefts, 8)
    return jnp.concatenate([exact_nn(small, rest) for small, rest in zip(smalls, rests)], axis=0)


def rotate_kernel(
    cells,
    hi, lo, total, singular, volumes,
    new_out, singular_out, hankel_out,
    rows_hi, rows_lo, result, root, in_sem, out_sem,
):
    tile, width = result.shape
    modes = 2 * tile
    snap_count = hi.shape[0] - modes
    near = tile + snap_count
    chunks = width // TURN
    core = lax.axis_index("mode")
    first_core = core == 0

    def piece(k):
        return pl.ds(pl.multiple_of(k * TURN, TURN), TURN)

    def loads(k):
        cols = piece(k)
        return (
            pltpu.make_async_copy(hi.at[:, cols], rows_hi.at[:, cols], in_sem.at[0, k]),
            pltpu.make_async_copy(lo.at[:, cols], rows_lo.at[:, cols], in_sem.at[1, k]),
        )

    for k in range(chunks):
        for copy in loads(k):
            copy.start()
    root[...] = lax.rsqrt(volumes[...] * (1.0 / cells))

    s = singular[...]
    s2 = s * s
    mid = tile // 2

    def get(which, row, count):
        flat = total.shape[2]
        first = row // flat
        return total[which, first : first + count // flat].reshape(count, tile)

    def both_cores(row, count):
        mine, others = get(0, row, count), get(1, row, count)
        return jnp.where(first_core, mine, others), jnp.where(first_core, others, mine)

    halves = both_cores(tile + mid, snap_count)
    project_t = jnp.concatenate(halves, axis=1)
    low_diagonal, low_corner = both_cores(0, mid), both_cores(mid, mid)
    snap_square = sum(value[:snap_count, mid : mid + snap_count] for value in low_corner)
    lower = jnp.concatenate(both_cores(tile, mid), axis=0)
    between = exact_nn(halves[1], lower)
    diagonal = jnp.zeros((snap_count, snap_count), f32)
    one_side = exact_nt(between, halves[0])
    for part, ends, corner in zip(halves, low_diagonal, low_corner):
        ahead, behind = part[:, :mid], part[:, mid:]
        diagonal += exact_nt(exact_nn(ahead, ends[:, :mid]), ahead)
        diagonal += exact_nt(exact_nn(behind, ends[:, mid:]), behind)
        one_side += exact_nt(exact_nn(behind, corner[:, :mid]), ahead)
    scaled_t = project_t * s2
    pad = jnp.zeros((tile - 2 * snap_count, modes), f32)
    turned = jnp.concatenate([project_t, scaled_t, pad], axis=0).T
    by_mode, by_mode_scaled = turned[:, :snap_count], turned[:, snap_count : 2 * snap_count]
    square = exact_nt(project_t, project_t)
    gram = (snap_square - 2.0 * square) + (diagonal + (one_side + one_side.T))
    pad = jnp.zeros((tile - 2 * snap_count, modes), f32)
    turned = jnp.concatenate([project_t, project_t * s2, pad], axis=0).T
    by_mode, by_mode_scaled = turned[:, :snap_count], turned[:, snap_count : 2 * snap_count]
    side = by_mode_scaled + exact_nn(by_mode, square + gram)
    side_and_project = jnp.concatenate([side, by_mode], axis=1)
    mine = own_inverse(project_t, s2, gram, first_core)
    both = exact_nn(mine, side_and_project)
    on_snaps = both[:, snap_count:]
    on_modes = mine * s2
    image = (on_modes + exact_nn(on_snaps, project_t)) * s
    energy = exact_nt(jnp.ones((8, modes), f32), image * image) + exact_nt(
        jnp.ones((8, snap_count), f32), both[:, :snap_count] * both[:, :snap_count]
    )
    singular_out[...] = jnp.sqrt(energy[:1])

    on_first, on_second = on_modes[:, :tile], on_modes[:, tile:]
    coef = split(
        jnp.concatenate(
            [
                jnp.where(first_core, on_first, on_second),
                on_snaps,
                jnp.where(first_core, on_second, on_first),
            ],
            axis=1,
        )
    )

    def rotate(k, carry):
        for copy in loads(k):
            copy.wait()
        cols = piece(k)
        value = dot3_nn(coef, (rows_hi[:, cols], rows_lo[:, cols]))
        result[:, cols] = value * root[:, cols]
        pltpu.make_async_copy(result.at[:, cols], new_out.at[:, cols], out_sem.at[k]).start()
        return carry

    lax.fori_loop(0, chunks, rotate, 0)

    base = tile + mid + snap_count
    swapped = (get(1, base + tile, tile), get(1, base + modes, snap_count), get(1, base, tile))
    straight = (get(0, base, tile), get(0, base + modes, snap_count), get(0, base + tile, tile))
    columns = jnp.concatenate(
        [
            jnp.concatenate(
                [jnp.where(first_core, a, b), jnp.where(first_core, b, a)], axis=1
            )
            for a, b in zip(straight, swapped)
        ],
        axis=0,
    )
    hankel_out[...] = dot3_nn(coef, split(columns))

    def finish(k, carry):
        pltpu.make_async_copy(result.at[:, piece(k)], new_out.at[:, piece(k)], out_sem.at[k]).wait()
        return carry

    lax.fori_loop(0, chunks, finish, 0)


def rotate(cells, hi, lo, total, singular, volumes):
    rows, width = hi.shape
    modes = singular.shape[1]
    tile = modes // 2
    chunks = width // TURN
    dma = pltpu.SemaphoreType.DMA
    vmem = pltpu.VMEM
    any_spec = pl.BlockSpec(memory_space=pl.ANY)
    vmem_spec = pl.BlockSpec(memory_space=vmem)
    return pl.pallas_call(
        functools.partial(rotate_kernel, cells),
        out_shape=(
            jax.ShapeDtypeStruct((tile, width), f32),
            jax.ShapeDtypeStruct((1, tile), f32),
            jax.ShapeDtypeStruct((tile, modes), f32),
        ),
        in_specs=[any_spec] * 2 + [vmem_spec] * 3,
        out_specs=(any_spec, vmem_spec, vmem_spec),
        scratch_shapes=[
            vmem((rows, width), bf16),
            vmem((rows, width), bf16),
            vmem((tile, width), f32),
            vmem((1, width), f32),
            dma((2, chunks)),
            dma((chunks,)),
        ],
        compiler_params=pltpu.CompilerParams(vmem_limit_bytes=56 * 1024 * 1024),
    )(hi, lo, total, singular, volumes)


def shards(basis, adjoint, snapshots, volumes, singular):
    tile, width = basis.shape
    cells = float(width * lax.axis_size("space"))
    volumes = volumes.reshape(1, width)
    hi, lo, total = gather(cells, basis, adjoint, snapshots, volumes)
    new_tile, new_singular, hankel = rotate(
        cells, hi, lo, total, singular.reshape(1, 2 * tile), volumes
    )
    return new_tile, new_singular.reshape(tile), hankel


def solution(mesh):
    return jax.shard_map(
        shards,
        mesh=mesh,
        in_specs=(P("mode", "space"), P("mode", "space"), P("mode", "space"), P("space"), P()),
        out_specs=(P("mode", "space"), P("mode"), P("mode", None)),
        check_vma=False,
    )
```
